32 devices in a mesh: section: 2 (over core), seq: 8 (over z, x), head: 2 (over y).
Axes of the slice: x: 2, y: 2, z: 4, core: 2. Of those that a mesh axis runs over, the one named last changes fastest.
Arguments:
- hidden_in: bfloat16 [4, 2048, 1024], P(None, 'seq'), may hold values from -6 to 6
- order: int32 [4], replicated, may hold values from 0 to 3, each once
- cotangent: bfloat16 [4, 2048, 1024], P(None, 'seq'), may hold values from -6 to 6
- norm_gain: float32 [2, 1024], P('section'), may hold values from 0.25 to 1.75
- w_z: bfloat16 [2, 1024, 2048], P('section', None, 'head'), may hold values from -0.1875 to 0.1875
- w_x: bfloat16 [2, 1024, 2048], P('section', None, 'head'), may hold values from -0.1875 to 0.1875
- w_bc: bfloat16 [2, 1024, 256], P('section'), may hold values from -0.1875 to 0.1875
- w_dt: bfloat16 [2, 1024, 32], P('section', None, 'head'), may hold values from -0.1875 to 0.1875
- dt_bias: float32 [2, 32], P('section', 'head'), may hold values from -12 to -3
- a_log: float32 [2, 32], P('section', 'head'), may hold values from -1 to 1
- d_skip: float32 [2, 32], P('section', 'head'), may hold values from 0.5 to 1.5
- conv_x: float32 [2, 4, 2048], P('section', None, 'head'), may hold values from -3 to 3
- conv_bias_x: float32 [2, 2048], P('section', 'head'), may hold values from -3 to 3
- conv_bc: float32 [2, 4, 256], P('section'), may hold values from -3 to 3
- conv_bias_bc: float32 [2, 256], P('section'), may hold values from -3 to 3
- mix_gain: float32 [2, 2048], P('section', 'head'), may hold values from 0.25 to 1.75
- w_out: bfloat16 [2, 2048, 1024], P('section', 'head'), may hold values from -0.125 to 0.125
Outputs:
- activations: bfloat16 [2, 4, 2048, 1024], P('section', None, 'seq')
- grads: float32 [2, 4, 2048, 1024], P('section', None, 'seq')
- grad_norm_gain: float32 [2, 1024], P('section')
- grad_w_z: float32 [2, 1024, 2048], P('section', None, 'head')
- grad_w_x: float32 [2, 1024, 2048], P('section', None, 'head')
- grad_w_bc: float32 [2, 1024, 256], P('section')
- grad_w_dt: float32 [2, 1024, 32], P('section', None, 'head')
- grad_dt_bias: float32 [2, 32], P('section', 'head')
- grad_a_log: float32 [2, 32], P('section', 'head')
- grad_d_skip: float32 [2, 32], P('section', 'head')
- grad_conv_x: float32 [2, 4, 2048], P('section', None, 'head')
- grad_conv_bias_x: float32 [2, 2048], P('section', 'head')
- grad_conv_bc: float32 [2, 4, 256], P('section')
- grad_conv_bias_bc: float32 [2, 256], P('section')
- grad_mix_gain: float32 [2, 2048], P('section', 'head')
- grad_w_out: float32 [2, 2048, 1024], P('section', 'head')
The draws below stay inside these ranges and needn't reach their ends.
Inputs may be any that keep to these rules, and one draw needn't show every extreme that they name: `order`: each micro-batch takes a different sequence.
All inputs are finite; a program needn't handle non-finite values.
Results may differ from the reference program's by a relative error of at most 0.019.
Values may be sent and summed in bfloat16 or wider, within the bound.
No kernel may reach another device: no remote copies, remote signals or barrier semaphores. Data moves between devices by JAX's collectives and lax.ppermute only.
A program may use at most 192 MiB of HBM per device.

```python
import math
import jax
import jax.numpy as jnp
from jax import lax

D = 1024
HEADS = 32
STATE = 128
KERNEL = 4
GROUP = 256
MICRO = 4
INNER = 2048
LENGTH = 2048


def draw_dt_bias(key, part):
    key = jax.random.fold_in(key, 7)
    lower_end = math.log(0.3 / LENGTH)
    upper_end = math.log(0.03)
    spread = jax.random.uniform(key, (2, HEADS), jnp.float32, lower_end, upper_end)
    target = jnp.exp(spread)
    return jnp.log(jnp.expm1(target))


def shard_levels(own_key, extent, split, smallest, largest):
    factor_of = 1.0
    for position, parts in split:
        draws = jax.random.uniform(jax.random.fold_in(jax.random.fold_in(own_key, 6), position), (parts,), jnp.float32, smallest / len(split), largest / len(split))
        factor_of = factor_of * jnp.repeat(jnp.exp(draws), extent[position] // parts).reshape((-1,) + (1,) * (len(extent) - 1 - position))
    return factor_of


def centred(rng, dims, scale, limit, pieces=(), held_as=jnp.bfloat16):
    result = jax.random.normal(rng, dims, jnp.float32) * scale
    if len(pieces) > 0:
        result = shard_levels(rng, dims, pieces, -0.22, 0.18) * result
    return jnp.clip(result, min=-limit, max=limit).astype(held_as)


def setup_inputs(seed: int = 0) -> dict:
    key_list = jax.random.split(jax.random.key(seed), 18)
    hidden_in = centred(key_list[0], (MICRO, LENGTH, D), 1.0, 6.0, ((1, 8),))
    order = jax.random.permutation(key_list[1], MICRO).astype(jnp.int32)
    cotangent = centred(key_list[2], (MICRO, LENGTH, D), 1.0, 6.0, ((1, 8),))
    norm_gain = jnp.clip(1.0 + 0.15 * jax.random.normal(key_list[3], (2, D), jnp.float32), 0.25, 1.75)
    w_z = centred(key_list[4], (2, D, INNER), D ** -0.5, 0.1875, ((0, 2), (2, 2)))
    w_x = centred(key_list[5], (2, D, INNER), D ** -0.5, 0.1875, ((0, 2), (2, 2)))
    w_bc = centred(key_list[6], (2, D, 2 * STATE), D ** -0.5, 0.1875, ((0, 2),))
    w_dt = centred(key_list[7], (2, D, HEADS), D ** -0.5, 0.1875, ((0, 2), (2, 2)))
    dt_bias = draw_dt_bias(jax.random.fold_in(key_list[17], 71), 0)
    a_log = jnp.clip(jax.random.uniform(key_list[9], (2, HEADS), jnp.float32, -1.0, 1.0) * shard_levels(key_list[9], (2, HEADS), ((0, 2), (1, 2)), -0.4, 0.0), -1.0, 1.0)
    d_skip = jnp.clip(0.5 + 1.0 * jax.random.uniform(key_list[10], (2, HEADS), jnp.float32) ** shard_levels(key_list[10], (2, HEADS), ((0, 2), (1, 2)), -0.2, 0.2), 0.5, 1.5)
    conv_x = centred(key_list[11], (2, KERNEL, INNER), KERNEL ** -0.5, 3.0, ((0, 2), (2, 2)), jnp.float32)
    conv_bias_x = centred(key_list[12], (2, INNER), 0.5, 3.0, ((0, 2), (1, 2)), jnp.float32)
    conv_bc = centred(key_list[13], (2, KERNEL, 2 * STATE), KERNEL ** -0.5, 3.0, ((0, 2),), jnp.float32)
    conv_bias_bc = centred(key_list[14], (2, 2 * STATE), 0.5, 3.0, ((0, 2),), jnp.float32)
    mix_gain = jnp.clip(1.0 + 0.15 * jax.random.normal(key_list[15], (2, INNER), jnp.float32), 0.25, 1.75)
    w_out = centred(key_list[16], (2, INNER, D), INNER ** -0.5, 0.125, ((0, 2), (1, 2)))
    return {"hidden_in": hidden_in, "order": order, "cotangent": cotangent, "norm_gain": norm_gain, "w_z": w_z, "w_x": w_x, "w_bc": w_bc, "w_dt": w_dt, "dt_bias": dt_bias, "a_log": a_log, "d_skip": d_skip, "conv_x": conv_x, "conv_bias_x": conv_bias_x, "conv_bc": conv_bc, "conv_bias_bc": conv_bias_bc, "mix_gain": mix_gain, "w_out": w_out}


@jax.custom_vjp
def low(v):
    return lax.optimization_barrier(v.astype(jnp.bfloat16)).astype(jnp.float32)

@jax.custom_vjp
def low_back(v):
    return v

def low_keep(v):
    return (low(v), None)

def low_pass(kept, grad):
    return (grad,)

def back_keep(v):
    return (v, None)

def back_low(kept, grad):
    return (low(grad),)
low.defvjp(low_keep, low_pass)
low_back.defvjp(back_keep, back_low)
EPS = 1e-05
HIGH = lax.Precision.HIGHEST

def exact(left, right):
    return jnp.dot(left, right, precision=HIGH, preferred_element_type=jnp.float32)

def ssd_block(start, block, skip):
    signal, write_key, read_key, step, decay_sum = block
    length = signal.shape[0]
    index = jnp.arange(length)
    lower = (index[:, None] >= index[None, :])[None]
    gram = exact(read_key, write_key.T)
    diff = decay_sum.T[:, :, None] - decay_sum.T[:, None, :]
    decay = jnp.where(lower, jnp.exp(jnp.where(lower, diff, 0.0)), 0.0)
    mixing = gram[None] * decay * step.T[:, None, :]
    intra = jnp.einsum('hts,shp->thp', mixing, signal, precision=HIGH)
    inter = jnp.exp(decay_sum)[:, :, None] * jnp.einsum('tn,hpn->thp', read_key, start, precision=HIGH)
    tail = jnp.exp(decay_sum[-1][None, :] - decay_sum) * step
    local = jnp.einsum('sh,shp,sn->hpn', tail, signal, write_key, precision=HIGH)
    after = jnp.exp(decay_sum[-1])[:, None, None] * start + local
    return (after, intra + inter + skip[None, :, None] * signal)

def layer(weights, wide_in):
    gain, w_gate, w_signal, w_keys, w_step, step_bias, log_rate, skip, conv_signal, bias_signal, conv_keys, bias_keys, mix_gain, w_out = weights
    length = wide_in.shape[0]
    inverse_rms = lax.rsqrt(lax.optimization_barrier(jnp.mean(wide_in * wide_in, -1, keepdims=True)) + EPS)
    normed = low(wide_in * inverse_rms * gain)
    gate_in = low_back(exact(normed, w_gate))
    signal_in = low_back(exact(normed, w_signal))
    keys_in = low_back(exact(normed, w_keys))
    step_raw = low_back(exact(normed, w_step))
    joined = jnp.concatenate([signal_in, keys_in], 1)
    kernel = jnp.concatenate([conv_signal, conv_keys], 1)
    kernel_bias = jnp.concatenate([bias_signal, bias_keys], 0)
    taps = kernel.shape[0]
    padded = jnp.concatenate([jnp.zeros((taps - 1, joined.shape[1]), jnp.float32), joined], 0)
    preact = kernel_bias + sum((kernel[offset] * padded[offset:offset + length] for offset in range(taps)))
    activated = jax.nn.silu(preact)
    inner = w_signal.shape[1]
    heads = w_step.shape[1]
    state = w_keys.shape[1] // 2
    width_head = inner // heads
    blocks = length // GROUP
    signal = activated[:, :inner].reshape(blocks, GROUP, heads, width_head)
    write_key = activated[:, inner:inner + state].reshape(blocks, GROUP, state)
    read_key = activated[:, inner + state:].reshape(blocks, GROUP, state)
    step = jax.nn.softplus(step_raw + step_bias)
    log_decay = -jnp.exp(log_rate) * step
    decay_sum = jnp.cumsum(log_decay.reshape(blocks, GROUP, heads), 1)
    step_blocks = step.reshape(blocks, GROUP, heads)
    body_fn = jax.checkpoint(lambda carry, block: ssd_block(carry, block, skip))
    _, outputs = lax.scan(body_fn, jnp.zeros((heads, width_head, state), jnp.float32), (signal, write_key, read_key, step_blocks, decay_sum))
    ssd_out = outputs.reshape(length, inner)
    gated = ssd_out * jax.nn.silu(gate_in)
    mix_scale = lax.rsqrt(lax.optimization_barrier(jnp.mean(gated * gated, -1, keepdims=True)) + EPS)
    mixed = low(gated * mix_scale * mix_gain)
    branch = low_back(exact(mixed, w_out))
    return wide_in + branch

def forward(weights, inputs, probe):
    first_layer = tuple((weight[0] for weight in weights))
    second_layer = tuple((weight[1] for weight in weights))
    middles = []
    finals = []
    for index in range(inputs.shape[0]):
        middle = low_back(low(layer(first_layer, inputs[index]))) + probe[index]
        middles.append(middle)
        finals.append(layer(second_layer, middle))
    return (jnp.stack(middles), jnp.stack(finals))

def reference(hidden_in, order, cotangent, norm_gain, w_z, w_x, w_bc, w_dt, dt_bias, a_log, d_skip, conv_x, conv_bias_x, conv_bc, conv_bias_bc, mix_gain, w_out):
    weights = tuple((weight.astype(jnp.float32) for weight in (norm_gain, w_z, w_x, w_bc, w_dt, dt_bias, a_log, d_skip, conv_x, conv_bias_x, conv_bc, conv_bias_bc, mix_gain, w_out)))
    inputs = jnp.take(hidden_in, order, axis=0).astype(jnp.float32)
    probe = jnp.zeros(inputs.shape, jnp.float32)
    (middles, finals), pullback = jax.vjp(forward, weights, inputs, probe)
    grad_weights, grad_inputs, grad_probe = pullback((jnp.zeros(middles.shape, jnp.float32), cotangent.astype(jnp.float32)))
    activations = jnp.stack([middles, finals]).astype(jnp.bfloat16)
    grads = jnp.stack([grad_inputs, grad_probe])
    return (activations, grads, grad_weights[0], grad_weights[1], grad_weights[2], grad_weights[3], grad_weights[4], grad_weights[5], grad_weights[6], grad_weights[7], grad_weights[8], grad_weights[9], grad_weights[10], grad_weights[11], grad_weights[12], grad_weights[13])
```

```python
import jax
import jax.numpy as jnp
from jax import lax
from jax.sharding import PartitionSpec as P

EPS = 1e-05
F32 = jnp.float32
BF16 = jnp.bfloat16


def exchange(block, axis, bit):
    route = [(i, i ^ bit) for i in range(lax.axis_size(axis))]
    return lax.ppermute(block, axis, route)


def shifted(block, axis, distance):
    devices = range(lax.axis_size(axis))
    route = [(i - distance, i) for i in devices if i - distance in devices]
    return lax.ppermute(block, axis, route)


def head_sum(part):
    bit = 1
    total = part.astype(F32)
    while bit < lax.axis_size("head"):
        low = total.astype(BF16)
        total = low.astype(F32) + exchange(low, "head", bit).astype(F32)
        bit *= 2
    return total


def head_sum_wide(total):
    bit = 1
    while bit < lax.axis_size("head"):
        total = total + exchange(total, "head", bit)
        bit *= 2
    return total


def matmul(left, right):
    return jnp.dot(left, right, preferred_element_type=F32)


def lead_dot(left, right):
    return lax.dot_general(
        left, right, (((0,), (0,)), ((), ())), preferred_element_type=F32
    )


def tail_dot(left, right):
    return lax.dot_general(
        left, right, (((1,), (1,)), ((), ())), preferred_element_type=F32
    )


def low(value):
    return value.astype(BF16)


def silu_slope(value):
    sigma = jax.nn.sigmoid(value)
    return sigma * (1.0 + value * (1.0 - sigma))


def send_chunks(chunks):
    me = lax.axis_index("seq")
    pick = lambda d: lax.dynamic_index_in_dim(chunks, me ^ d, 0, False)
    return [pick(0)] + [exchange(pick(d), "seq", d) for d in range(1, chunks.shape[0])]


def scan_states(fade, local, fades):
    blocks = lax.axis_size("seq")
    me = lax.axis_index("seq")
    reverse = fades is not None
    width, state = local.shape
    rows = width // blocks
    message = low(local).reshape(blocks, rows, state)
    if fades is None:
        heads = fade.shape[0]
        per = max(1, heads // blocks)
        spread = jnp.repeat(fade, blocks * per // heads).reshape(blocks, per, 1)
        high = low(spread).astype(F32)
        pair = jnp.concatenate([high, spread - high], 1)
        tail = jnp.pad(low(jnp.broadcast_to(pair, (blocks, 2 * per, state))), ((0, 0), (0, 16 - 2 * per), (0, 0)))
        message = jnp.concatenate([message, tail], 1)
    arrived = jnp.stack(send_chunks(message))
    if fades is None:
        fades = (arrived[:, rows : rows + per].astype(F32) + arrived[:, rows + per : rows + 2 * per].astype(F32))
        arrived = arrived[:, :rows]
    per = fades.shape[1]
    running = jnp.zeros((rows, state), F32)
    entering = []
    order = range(blocks - 1, -1, -1) if reverse else range(blocks)
    for block in order:
        entering.append(low(running))
        one = lax.dynamic_index_in_dim(arrived, me ^ block, 0, False).astype(F32)
        factor = lax.dynamic_index_in_dim(fades, me ^ block, 0, False)
        running = (running.reshape(per, rows // per, state) * factor[:, None, :]).reshape(rows, state) + one
    if reverse:
        entering = entering[::-1]
    returned = send_chunks(jnp.stack(entering))
    returned = jnp.stack(returned)
    ordered = jnp.stack(
        [lax.dynamic_index_in_dim(returned, me ^ block, 0, False) for block in range(blocks)]
    )
    return ordered.reshape(width, state), fades


def by_head(values, width):
    return jnp.repeat(values, width, axis=1)


def of_heads(values, heads):
    return jnp.sum(values.reshape(values.shape[0], heads, -1), 2)


def conv_preact(weights, padded, length):
    kernel = jnp.concatenate([weights["conv_x"], weights["conv_bc"]], 1)
    bias = jnp.concatenate([weights["conv_bias_x"], weights["conv_bias_bc"]], 0)
    taps = kernel.shape[0]
    return kernel, bias + sum(
        kernel[offset] * padded[offset : offset + length] for offset in range(taps)
    )


def ssd_parts(weights, preact, step_raw):
    activated = jax.nn.silu(preact)
    inner = weights["w_x"].shape[1]
    state = weights["w_bc"].shape[1] // 2
    length = preact.shape[0]
    signal = activated[:, :inner]
    write_key = activated[:, inner : inner + state]
    read_key = activated[:, inner + state :]
    step = jax.nn.softplus(step_raw + weights["dt_bias"])
    rate = -jnp.exp(weights["a_log"])
    decay_sum = jnp.cumsum(rate * step, 0)
    index = jnp.arange(length)
    lower = (index[:, None] >= index[None, :])[None]
    diff = decay_sum.T[:, :, None] - decay_sum.T[:, None, :]
    decay = jnp.where(lower, jnp.exp(jnp.where(lower, diff, 0.0)), 0.0)
    gram = tail_dot(low(read_key), low(write_key))
    return signal, write_key, read_key, step, rate, decay_sum, decay, gram


def layer_forward(entry, weights):
    length = entry.shape[0]
    wide = entry.astype(F32)
    inverse_rms = lax.rsqrt(jnp.mean(wide * wide, -1, keepdims=True) + EPS)
    normed = low(wide * inverse_rms * weights["norm_gain"])
    joined = jnp.concatenate([matmul(normed, weights["w_x"]), matmul(normed, weights["w_bc"])], 1)
    step_raw = matmul(normed, weights["w_dt"])
    taps = weights["conv_x"].shape[0]
    before = shifted(joined[length - taps + 1 :], "seq", 1)
    gate_in = matmul(normed, weights["w_z"])
    padded = jnp.concatenate([before, joined], 0)
    _, preact = conv_preact(weights, padded, length)
    signal, write_key, read_key, step, rate, decay_sum, decay, gram = ssd_parts(
        weights, preact, step_raw
    )
    heads = step.shape[1]
    inner = signal.shape[1]
    width = inner // heads
    tail = jnp.exp(decay_sum[-1][None, :] - decay_sum) * step
    local = lead_dot(low(by_head(tail, width) * signal), low(write_key))
    start, fades = scan_states(jnp.exp(decay_sum[-1]), local, None)
    mixing = gram[None] * decay * step.T[:, None, :]
    intra = jnp.einsum(
        "hts,shp->thp", low(mixing), low(signal).reshape(length, heads, width),
        preferred_element_type=F32,
    ).reshape(length, inner)
    inter = by_head(jnp.exp(decay_sum), width) * tail_dot(low(read_key), start)
    ssd_out = intra + inter + jnp.repeat(weights["d_skip"], width) * signal
    gated = ssd_out * jax.nn.silu(gate_in)
    total_inner = inner * lax.axis_size("head")
    squares = head_sum_wide(jnp.sum(gated * gated, -1))
    mix_scale = lax.rsqrt(squares / total_inner + EPS)[:, None]
    branch = mix_scale * head_sum(matmul(low(gated * weights["mix_gain"]), weights["w_out"]))
    kept = (entry, inverse_rms, normed, gate_in, padded, step_raw, start, fades, ssd_out, mix_scale, branch)
    return low(wide + branch), kept


def layer_backward(grad_out, kept, weights):
    entry, inverse_rms, normed, gate_in, padded, step_raw, start, fades, ssd_out, mix_scale, branch = kept
    length = entry.shape[0]
    wide_grad = grad_out.astype(F32)
    grad_low = low(grad_out)
    gated = ssd_out * jax.nn.silu(gate_in)
    mixed = low(gated * mix_scale * weights["mix_gain"])
    grad_mixed = tail_dot(grad_low, weights["w_out"])
    grad_mix_gain = jnp.sum(grad_mixed * gated * mix_scale, 0)
    weighted = grad_mixed * weights["mix_gain"]
    inner = gated.shape[1]
    total_inner = inner * lax.axis_size("head")
    along = jnp.sum(grad_low.astype(F32) * branch, -1, keepdims=True)
    grad_gated = mix_scale * weighted - gated * (mix_scale**2 * along / total_inner)
    grad_y = grad_gated * jax.nn.silu(gate_in)
    gate_low = low(grad_gated * ssd_out * silu_slope(gate_in))
    kernel, preact = conv_preact(weights, padded, length)
    signal, write_key, read_key, step, rate, decay_sum, decay, gram = ssd_parts(
        weights, preact, step_raw
    )
    heads = step.shape[1]
    width = inner // heads
    write_low, read_low = low(write_key), low(read_key)
    rise = jnp.exp(decay_sum)
    grad_reach = low(grad_y * by_head(rise, width))
    grad_start = lead_dot(grad_reach, read_low)
    grad_local, _ = scan_states(None, grad_start, fades)
    grad_skip = jnp.sum(of_heads(grad_y * signal, heads), 0)
    cube = lambda a: low(a).reshape(length, heads, width)
    base = decay * step.T[:, None, :]
    mixing = gram[None] * base
    grad_signal = jnp.repeat(weights["d_skip"], width) * grad_y + jnp.einsum(
        "hts,thp->shp", low(mixing), cube(grad_y), preferred_element_type=F32
    ).reshape(length, inner)
    grad_mixing = jnp.einsum("thp,shp->hts", cube(grad_y), cube(signal), preferred_element_type=F32)
    grad_gram = low(jnp.sum(grad_mixing * base, 0))
    grad_read = matmul(grad_gram, write_low) + matmul(grad_reach, start)
    grad_write = lead_dot(grad_gram, read_low)
    grad_log = grad_mixing * mixing
    grad_decay_sum = (jnp.sum(grad_log, 2) - jnp.sum(grad_log, 1)).T
    grad_step = jnp.sum(grad_mixing * gram[None] * decay, 1).T
    reach = tail_dot(read_low, start)
    grad_decay_sum = grad_decay_sum + of_heads(grad_y * reach, heads) * rise
    fade = rise[-1]
    last_row = (jnp.arange(length) == length - 1)[:, None]
    products = jnp.sum(grad_local.astype(F32) * start.astype(F32), 1).reshape(heads, width)
    grad_decay_sum = grad_decay_sum + jnp.where(last_row, (jnp.sum(products, 1) * fade)[None, :], 0.0)
    keep = jnp.exp(decay_sum[-1][None, :] - decay_sum)
    tail = keep * step
    spread = tail_dot(write_low, grad_local)
    wide_tail = by_head(tail, width)
    grad_signal = grad_signal + wide_tail * spread
    grad_write = grad_write + matmul(low(wide_tail * signal), grad_local)
    grad_tail = of_heads(signal * spread, heads)
    grad_step = grad_step + grad_tail * keep
    grad_tail_log = grad_tail * tail
    grad_decay_sum = (
        grad_decay_sum
        - grad_tail_log
        + jnp.where(last_row, jnp.sum(grad_tail_log, 0)[None, :], 0.0)
    )
    grad_log_step = jnp.flip(jnp.cumsum(jnp.flip(grad_decay_sum, 0), 0), 0)
    grad_log_rate = jnp.sum(grad_log_step * step, 0) * rate
    grad_step = grad_step + grad_log_step * rate
    grad_step_raw = grad_step * jax.nn.sigmoid(step_raw + weights["dt_bias"])
    grad_step_bias = jnp.sum(grad_step_raw, 0)
    grad_pre = jnp.concatenate([grad_signal, grad_write, grad_read], 1) * silu_slope(preact)
    taps = kernel.shape[0]
    grad_kernel = jnp.stack(
        [jnp.sum(grad_pre * padded[offset : offset + length], 0) for offset in range(taps)]
    )
    grad_kernel_bias = jnp.sum(grad_pre, 0)
    after = shifted(grad_pre[: taps - 1], "seq", -1)
    extended = jnp.concatenate([grad_pre, after], 0)
    grad_joined = sum(
        kernel[offset] * extended[taps - 1 - offset : taps - 1 - offset + length]
        for offset in range(taps)
    )
    signal_low = low(grad_joined[:, :inner])
    keys_low = low(grad_joined[:, inner:])
    step_low = low(grad_step_raw)
    grad_normed = head_sum(
        tail_dot(gate_low, weights["w_z"])
        + tail_dot(signal_low, weights["w_x"])
        + tail_dot(keys_low, weights["w_bc"])
        + tail_dot(step_low, weights["w_dt"])
    )
    wide = entry.astype(F32)
    grad_gain = jnp.sum(grad_normed * wide * inverse_rms, 0)
    scaled = grad_normed * weights["norm_gain"]
    grad_in = inverse_rms * scaled - wide * inverse_rms**3 * jnp.mean(
        scaled * wide, -1, keepdims=True
    )
    factors = (mixed, grad_low, normed, gate_low, signal_low, keys_low, step_low)
    vectors = (
        grad_gain,
        grad_step_bias,
        grad_log_rate,
        grad_skip,
        grad_kernel[:, :inner],
        grad_kernel_bias[:inner],
        grad_kernel[:, inner:],
        grad_kernel_bias[inner:],
        grad_mix_gain,
    )
    return wide_grad + grad_in, factors, vectors


NAMES = (
    "norm_gain",
    "w_z",
    "w_x",
    "w_bc",
    "w_dt",
    "dt_bias",
    "a_log",
    "d_skip",
    "conv_x",
    "conv_bias_x",
    "conv_bc",
    "conv_bias_bc",
    "mix_gain",
    "w_out",
)


def both_layers(mine):
    first = lax.axis_index("section") == 0
    other = {}
    for name in ("w_x", "w_bc", "w_dt", "w_z", "w_out"):
        other[name] = exchange(mine[name], "section", 1)
    vectors = [name for name in NAMES if not name.startswith("w_")]
    flat = jnp.concatenate([mine[name].reshape(-1) for name in vectors])
    flat = exchange(flat, "section", 1)
    place = 0
    for name in vectors:
        size = mine[name].size
        other[name] = flat[place : place + size].reshape(mine[name].shape)
        place += size
    layer = lambda flag: {name: jnp.where(flag, mine[name], other[name]) for name in NAMES}
    return layer(first), layer(~first)


def shards(hidden_in, order, cotangent, *params):
    mine = {name: param[0] for name, param in zip(NAMES, params)}
    layers = both_layers(mine)
    sections = lax.axis_size("section")
    section = lax.axis_index("section")
    count = order.shape[0] // sections
    base = section * count
    entries = [
        lax.dynamic_index_in_dim(hidden_in, order[base + index], 0, False) for index in range(count)
    ]
    outputs = []
    kept = []
    for weights in layers:
        done = [layer_forward(entry, weights) for entry in entries]
        entries = [one[0] for one in done]
        outputs.append(jnp.stack(entries))
        kept.append([one[1] for one in done])
    cotangents = lax.dynamic_slice_in_dim(cotangent, base, count, 0)
    incoming = [cotangents[index] for index in range(count)]
    grads = [None, None]
    sums = [None, None]
    for layer in (1, 0):
        done = [layer_backward(incoming[index], kept[layer][index], layers[layer]) for index in range(count)]
        grads[layer] = jnp.stack([one[0] for one in done])
        incoming = [low(one[0]) for one in done]
        mixed, grad_low, normed, gate_low, signal_low, keys_low, step_low = (
            jnp.concatenate(parts, 0) for parts in zip(*(one[1] for one in done))
        )
        vectors = jax.tree.map(lambda *parts: sum(parts), *(one[2] for one in done))
        sums[layer] = {
            "w_out": lead_dot(mixed, grad_low),
            "w_z": lead_dot(normed, gate_low),
            "w_x": lead_dot(normed, signal_low),
            "w_bc": lead_dot(normed, keys_low),
            "w_dt": lead_dot(normed, step_low),
        }
        names = [name for name in NAMES if not name.startswith("w_")]
        sums[layer].update(zip(names, vectors))

    first = section == 0

    def to_owner(early, late):
        own = jnp.where(first, early, late)
        sent = exchange(jnp.where(first, late, early), "section", 1)
        return jnp.concatenate(
            [jnp.where(first, own, sent), jnp.where(first, sent, own)], 0
        )

    activations = to_owner(outputs[0], outputs[1])[None]
    grads = to_owner(grads[0], grads[1])[None]

    def reduced(name):
        own = jnp.where(first, sums[0][name], sums[1][name])
        sent = low(jnp.where(first, sums[1][name], sums[0][name]))
        total = low(own + exchange(sent, "section", 1).astype(F32))
        axes = ("seq", "head") if name in ("w_bc", "conv_bc", "conv_bias_bc") else "seq"
        return lax.psum(total, axes)

    return (activations, grads) + tuple(reduced(name).astype(F32)[None] for name in NAMES)


def solution(mesh):
    in_specs = (
        P(None, "seq", None),
        P(),
        P(None, "seq", None),
        P("section", None),
        P("section", None, "head"),
        P("section", None, "head"),
        P("section", None, None),
        P("section", None, "head"),
        P("section", "head"),
        P("section", "head"),
        P("section", "head"),
        P("section", None, "head"),
        P("section", "head"),
        P("section", None, None),
        P("section", None),
        P("section", "head"),
        P("section", "head", None),
    )
    out_specs = (
        P("section", None, "seq", None),
        P("section", None, "seq", None),
        P("section", None),
        P("section", None, "head"),
        P("section", None, "head"),
        P("section", None, None),
        P("section", None, "head"),
        P("section", "head"),
        P("section", "head"),
        P("section", "head"),
        P("section", None, "head"),
        P("section", "head"),
        P("section", None, None),
        P("section", None),
        P("section", "head"),
        P("section", "head", None),
    )
    return jax.shard_map(shards, mesh=mesh, in_specs=in_specs, out_specs=out_specs, check_vma=False)
```

```python
import functools

import jax
import jax.numpy as jnp
from jax import lax
from jax.experimental import pallas as pl
from jax.experimental.pallas import tpu as pltpu
from jax.sharding import PartitionSpec as P

EPS = 1e-05
F32 = jnp.float32
BF16 = jnp.bfloat16
LANES = 128
HALO = 8
VMEM = 24 * 1024 * 1024


def exchange(block, axis, bit):
    route = [(i, i ^ bit) for i in range(lax.axis_size(axis))]
    return lax.ppermute(block, axis, route)


def shifted(block, axis, distance):
    devices = range(lax.axis_size(axis))
    route = [(i - distance, i) for i in devices if i - distance in devices]
    return lax.ppermute(block, axis, route)


def low(value):
    return value.astype(BF16)


def wide(value):
    return value.astype(F32)


def matmul(left, right):
    return jnp.dot(left, right, preferred_element_type=F32)


def lead_dot(left, right):
    return lax.dot_general(left, right, (((0,), (0,)), ((), ())), preferred_element_type=F32)


def tail_dot(left, right):
    return lax.dot_general(left, right, (((1,), (1,)), ((), ())), preferred_element_type=F32)


def head_sum(part):
    bit = 1
    while bit < lax.axis_size("head"):
        part = low(part)
        part = wide(part) + wide(exchange(part, "head", bit))
        bit *= 2
    return part


def parts_of(value, count):
    terms = []
    for _ in range(count):
        term = low(value)
        terms.append(term)
        value = value - wide(term)
    return terms


def dot_parts(left, right, count, dot=matmul):
    return sum(dot(left, term) for term in parts_of(right, count))


def iota(shape, axis):
    return lax.broadcasted_iota(jnp.int32, shape, axis)


def lower_mask(length):
    return iota((length, length), 0) >= iota((length, length), 1)


def expand(values, pair):
    length = values.shape[0]
    early = iota((length, LANES), 1) < LANES // 2
    first = values[:, 2 * pair : 2 * pair + 1]
    second = values[:, 2 * pair + 1 : 2 * pair + 2]
    return jnp.where(early, first, second)


def head_matrix(inner, width):
    return jnp.where(iota((inner, LANES), 0) // width == iota((inner, LANES), 1), 1.0, 0.0).astype(BF16)


def head_sums(values, matrix):
    high, rest = parts_of(values, 2)
    return matmul(high, matrix) + matmul(rest, matrix)


def sigmoid(value):
    return 1.0 / (1.0 + jnp.exp(-value))


def softplus(value):
    tail = jnp.exp(-jnp.abs(value))
    shifted_one = 1.0 + tail
    gap = shifted_one - 1.0
    small = jnp.where(gap == 0.0, tail, jnp.log(shifted_one) * (tail / jnp.where(gap == 0.0, 1.0, gap)))
    return jnp.maximum(value, 0.0) + small


def conv_preact(joined_ref, before_ref, conv_ref, ext_ref):
    length, channels = joined_ref.shape[0], conv_ref.shape[1]
    ext_ref[0:HALO, :] = before_ref[...]
    ext_ref[HALO : HALO + length, :] = joined_ref[:, 0:channels]
    total = conv_ref[4:5, :]
    for tap in range(4):
        total = total + conv_ref[tap : tap + 1, :] * ext_ref[HALO - 3 + tap : HALO - 3 + tap + length, :]
    return total


def decays(joined_ref, head_ref, channels):
    length = joined_ref.shape[0]
    raw = joined_ref[:, channels : channels + LANES] + head_ref[0:1, :]
    step = softplus(raw)
    rate = -jnp.exp(head_ref[1:2, :])
    lower = jnp.where(lower_mask(length), 1.0, 0.0).astype(BF16)
    decay_sum = dot_parts(lower, rate * step, 3)
    return raw, step, rate, decay_sum


def pair_dots(early, mixing_a, mixing_b, values, dot):
    return jnp.where(early, dot(mixing_a, values), dot(mixing_b, values))


def local_kernel(joined_ref, before_ref, conv_ref, head_ref, y_ref, message_ref, read_ref, rise_ref, ext_ref, act_ref):
    length = joined_ref.shape[0]
    channels = conv_ref.shape[1]
    inner = y_ref.shape[1]
    state = read_ref.shape[1]
    pairs = inner // LANES
    preact = conv_preact(joined_ref, before_ref, conv_ref, ext_ref)
    act_ref[...] = preact * sigmoid(preact)
    write_low = low(act_ref[:, inner : inner + state])
    read_low = low(act_ref[:, inner + state : inner + 2 * state])
    read_ref[...] = read_low
    _, step, _, decay_sum = decays(joined_ref, head_ref, channels)
    rise_ref[...] = jnp.exp(decay_sum)
    keep_step = jnp.exp(decay_sum[length - 1 : length, :] - decay_sum) * step
    decay_rows = decay_sum.T
    step_rows = step.T
    gram = tail_dot(read_low, write_low)
    lower = lower_mask(length)
    early = iota((length, LANES), 1) < LANES // 2
    half = inner // 2
    for pair in range(pairs):
        lanes = slice(pair * LANES, (pair + 1) * LANES)
        signal = act_ref[:, lanes]
        signal_low = low(signal)
        mixings = []
        for head in (2 * pair, 2 * pair + 1):
            diff = decay_sum[:, head : head + 1] - decay_rows[head : head + 1, :]
            decay = jnp.exp(jnp.where(lower, diff, -1e30))
            mixings.append(low(gram * decay * step_rows[head : head + 1, :]))
        mixed = pair_dots(early, mixings[0], mixings[1], signal_low, matmul)
        y_ref[:, lanes] = mixed + conv_ref[5:6, lanes] * signal
        local = lead_dot(low(expand(keep_step, pair) * signal), write_low)
        place = pair * LANES
        if half % LANES == 0:
            side, row = place // half, place % half
            message_ref[side, row : row + LANES, :] = low(local)
    heads = 2 * pairs
    per = heads // 2
    for side in range(2):
        column = jnp.exp(decay_rows[side * per : side * per + 8, length - 1 : length])
        fade = jnp.broadcast_to(column, (8, state))
        high = wide(low(fade))
        message_ref[side, half : half + 16, :] = low(jnp.concatenate([high, fade - high], 0))


def output_kernel(y_ref, read_ref, rise_ref, start_ref, gate_ref, mix_ref, w_ref, ssd_ref, part_ref, mixed_ref):
    length, inner = y_ref.shape
    features = w_ref.shape[1]
    squares = jnp.zeros((length, 1), F32)
    for pair in range(inner // LANES):
        lanes = slice(pair * LANES, (pair + 1) * LANES)
        reach = tail_dot(read_ref[...], start_ref[lanes, :])
        ssd_out = y_ref[:, lanes] + expand(rise_ref[...], pair) * reach
        ssd_ref[:, lanes] = ssd_out
        gate = gate_ref[:, lanes]
        gated = ssd_out * (gate * sigmoid(gate))
        squares = squares + jnp.sum(gated * gated, 1, keepdims=True)
        mixed_ref[:, lanes] = low(gated * mix_ref[0:1, lanes])
    part_ref[:, 0:features] = low(matmul(mixed_ref[...], w_ref[...]))
    high = wide(low(squares))
    lane = iota((length, LANES), 1)
    tail = jnp.where(lane == 0, high, jnp.where(lane == 1, squares - high, 0.0))
    part_ref[:, features : features + LANES] = low(tail)


def gate_back_kernel(
    total_inner, grad_ref, w_ref, ssd_ref, gate_ref, scale_ref, branch_ref, mix_ref, rise_ref, read_ref,
    grad_y_ref, gate_low_ref, mixed_ref, start_ref, sums_ref,
):
    length, inner = ssd_ref.shape
    scale = scale_ref[:, 0:1]
    along = jnp.sum(wide(grad_ref[...]) * branch_ref[...], 1, keepdims=True) * (scale * scale / total_inner)
    half = inner // 2
    sums_ref[...] = jnp.zeros(sums_ref.shape, F32)
    for pair in range(inner // LANES):
        lanes = slice(pair * LANES, (pair + 1) * LANES)
        grad_mixed = tail_dot(grad_ref[...], w_ref[lanes, :])
        gain = mix_ref[0:1, lanes]
        gate = gate_ref[:, lanes]
        ssd_out = ssd_ref[:, lanes]
        sigma = sigmoid(gate)
        active = gate * sigma
        gated = ssd_out * active
        normal = gated * scale
        sums_ref[0:1, lanes] = jnp.sum(grad_mixed * normal, 0, keepdims=True)
        mixed_ref[:, lanes] = low(normal * gain)
        grad_gated = scale * (grad_mixed * gain) - gated * along
        grad_y = grad_gated * active
        grad_y_ref[:, lanes] = grad_y
        gate_low_ref[:, lanes] = low(grad_gated * ssd_out * (sigma * (1.0 + gate * (1.0 - sigma))))
        grad_reach = low(grad_y * expand(rise_ref[...], pair))
        grad_start = lead_dot(grad_reach, read_ref[...])
        place = pair * LANES
        if half % LANES == 0:
            side, row = place // half, place % half
            start_ref[side, row : row + LANES, :] = low(grad_start)


def scan_back_kernel(
    joined_ref, before_ref, conv_ref, head_ref, grad_y_ref, start_ref,
    signal_ref, keys_ref, sums_ref, row_ref,
    ext_ref, act_ref, step_ref, gram_ref, prod_ref,
):
    length, inner = grad_y_ref.shape
    channels = conv_ref.shape[1]
    state = start_ref.shape[1]
    pairs = inner // LANES
    preact = conv_preact(joined_ref, before_ref, conv_ref, ext_ref)
    act_ref[...] = preact * sigmoid(preact)
    write_low = low(act_ref[:, inner : inner + state])
    read_low = low(act_ref[:, inner + state : inner + 2 * state])
    _, step, _, decay_sum = decays(joined_ref, head_ref, channels)
    rise = jnp.exp(decay_sum)
    decay_rows = decay_sum.T
    step_rows = step.T
    gram = tail_dot(read_low, write_low)
    lower = lower_mask(length)
    early = iota((length, LANES), 1) < LANES // 2
    lane = iota((length, LANES), 1)
    step_ref[...] = jnp.zeros(step_ref.shape, F32)
    gram_ref[...] = jnp.zeros(gram_ref.shape, F32)
    columns = jnp.zeros((length, LANES), F32)
    grad_read = jnp.zeros((length, state), F32)
    row_ref[...] = jnp.zeros(row_ref.shape, F32)
    for pair in range(pairs):
        lanes = slice(pair * LANES, (pair + 1) * LANES)
        signal = act_ref[:, lanes]
        signal_low = low(signal)
        grad_y = grad_y_ref[:, lanes]
        grad_y_low = low(grad_y)
        mixings = []
        for head in (2 * pair, 2 * pair + 1):
            mine = early if head % 2 == 0 else jnp.logical_not(early)
            own = jnp.where(mine, grad_y, 0.0)
            grad_mixing = tail_dot(low(own), signal_low)
            diff = decay_sum[:, head : head + 1] - decay_rows[head : head + 1, :]
            decay = jnp.exp(jnp.where(lower, diff, -1e30))
            step_row = step_rows[head : head + 1, :]
            plain = gram * decay
            mixings.append(low(plain * step_row))
            gram_ref[...] += grad_mixing * decay * step_row
            weighed = grad_mixing * plain
            step_ref[head : head + 1, :] = jnp.sum(weighed, 0, keepdims=True)
            columns = jnp.where(lane == head, jnp.sum(weighed * step_row, 1, keepdims=True), columns)
        back = pair_dots(early, mixings[0], mixings[1], grad_y_low, lead_dot)
        signal_ref[:, lanes] = conv_ref[5:6, lanes] * grad_y + back
        row_ref[0:1, lanes] = jnp.sum(grad_y * signal, 0, keepdims=True)
        start = start_ref[lanes, :]
        reach = tail_dot(read_low, start)
        prod_ref[:, lanes] = grad_y * reach
        grad_read = grad_read + matmul(low(grad_y * expand(rise, pair)), start)
    gram_parts = parts_of(gram_ref[...], 2)
    keys_ref[:, 0:state] = sum(lead_dot(part, read_low) for part in gram_parts)
    keys_ref[:, state : 2 * state] = grad_read + sum(matmul(part, write_low) for part in gram_parts)
    grad_step = step_ref[...].T
    matrix = head_matrix(inner, LANES // 2)
    sums_ref[:, 0:LANES] = columns - step * grad_step + head_sums(prod_ref[...], matrix) * rise
    sums_ref[:, LANES : 2 * LANES] = grad_step


def state_back_kernel(
    joined_ref, before_ref, conv_ref, head_ref, signal_ref, keys_ref, sums_ref, local_ref, start_ref,
    pre_ref, raw_ref, conv_sums_ref, head_sums_ref,
    ext_ref, prod_ref,
):
    length, inner = signal_ref.shape
    channels = conv_ref.shape[1]
    state = start_ref.shape[1]
    preact = conv_preact(joined_ref, before_ref, conv_ref, ext_ref)
    raw, step, rate, decay_sum = decays(joined_ref, head_ref, channels)
    keep = jnp.exp(decay_sum[length - 1 : length, :] - decay_sum)
    tail = keep * step
    sigma = sigmoid(preact)
    active = preact * sigma
    slope = sigma * (1.0 + preact * (1.0 - sigma))
    write_low = low(active[:, inner : inner + state])
    grad_write = keys_ref[:, 0:state]
    conv_sums_ref[...] = jnp.zeros(conv_sums_ref.shape, F32)

    def finish(grad, lanes):
        grad_pre = grad * slope[:, lanes]
        pre_ref[:, lanes] = grad_pre
        for tap in range(4):
            rows = ext_ref[HALO - 3 + tap : HALO - 3 + tap + length, lanes]
            conv_sums_ref[tap : tap + 1, lanes] = jnp.sum(grad_pre * rows, 0, keepdims=True)
        conv_sums_ref[4:5, lanes] = jnp.sum(grad_pre, 0, keepdims=True)

    for pair in range(inner // LANES):
        lanes = slice(pair * LANES, (pair + 1) * LANES)
        signal = active[:, lanes]
        local = local_ref[lanes, :]
        spread = tail_dot(write_low, local)
        wide_tail = expand(tail, pair)
        prod_ref[:, lanes] = signal * spread
        grad_write = grad_write + matmul(low(wide_tail * signal), local)
        finish(signal_ref[:, lanes] + wide_tail * spread, lanes)
    finish(grad_write, slice(inner, inner + state))
    finish(keys_ref[:, state : 2 * state], slice(inner + state, inner + 2 * state))
    matrix = head_matrix(inner, LANES // 2)
    grad_tail = head_sums(prod_ref[...], matrix)
    grad_step = sums_ref[:, LANES : 2 * LANES] + grad_tail * keep
    tail_log = grad_tail * tail
    product = wide(local_ref[...]) * wide(start_ref[...])
    by_state = sum(lead_dot(matrix, part) for part in parts_of(product, 2))
    ones = jnp.ones((8, state), BF16)
    totals = sum(tail_dot(ones, part) for part in parts_of(by_state, 2))[0:1, :]
    fade = jnp.exp(decay_sum[length - 1 : length, :])
    last = iota((length, LANES), 0) == length - 1
    extra = jnp.sum(tail_log, 0, keepdims=True) + totals * fade
    grad_decay = sums_ref[:, 0:LANES] - tail_log + jnp.where(last, extra, 0.0)
    upper = jnp.where(iota((length, length), 1) >= iota((length, length), 0), 1.0, 0.0).astype(BF16)
    grad_log = dot_parts(upper, grad_decay, 3)
    grad_step = grad_step + grad_log * rate
    grad_raw = grad_step * sigmoid(raw)
    raw_ref[...] = low(grad_raw)
    head_sums_ref[...] = jnp.zeros(head_sums_ref.shape, F32)
    head_sums_ref[0:1, :] = jnp.sum(grad_raw, 0, keepdims=True)
    head_sums_ref[1:2, :] = jnp.sum(grad_log * step, 0, keepdims=True) * rate


def input_back_kernel(pre_ref, after_ref, conv_ref, raw_ref, gate_ref, w_ref, w_gate_ref, joined_ref, part_ref, ext_ref):
    length, channels = pre_ref.shape
    ext_ref[0:length, :] = pre_ref[...]
    ext_ref[length : length + HALO, :] = after_ref[...]
    total = jnp.zeros((length, channels), F32)
    for tap in range(4):
        total = total + conv_ref[tap : tap + 1, :] * ext_ref[3 - tap : 3 - tap + length, :]
    joined_ref[:, 0:channels] = low(total)
    joined_ref[:, channels : channels + LANES] = raw_ref[...]
    part_ref[...] = low(tail_dot(joined_ref[...], w_ref[...]) + tail_dot(gate_ref[...], w_gate_ref[...]))


def normalized(value, gain):
    return low(value * lax.rsqrt(jnp.mean(value * value, 1, keepdims=True) + EPS) * gain)


def merge_kernel(total_inner, part_ref, other_ref, entry_ref, gain_ref, out_ref, branch_ref, scale_ref, normed_ref):
    features = entry_ref.shape[1]
    total = wide(part_ref[...]) + wide(other_ref[...])
    squares = jnp.sum(total[:, features:], 1, keepdims=True)
    scale = lax.rsqrt(squares / total_inner + EPS)
    branch = scale * total[:, :features]
    out = low(wide(entry_ref[...]) + branch)
    out_ref[...] = out
    branch_ref[...] = branch
    scale_ref[...] = jnp.broadcast_to(scale, scale_ref.shape)
    normed_ref[...] = normalized(wide(out), gain_ref[0:1, :])


def entry_back_kernel(part_ref, other_ref, entry_ref, gain_ref, grad_ref, out_ref, low_ref, sums_ref):
    grad_normed = wide(part_ref[...]) + wide(other_ref[...])
    value = wide(entry_ref[...])
    inverse_rms = lax.rsqrt(jnp.mean(value * value, 1, keepdims=True) + EPS)
    sums_ref[...] = jnp.zeros(sums_ref.shape, F32)
    sums_ref[0:1, :] = jnp.sum(grad_normed * value * inverse_rms, 0, keepdims=True)
    scaled = grad_normed * gain_ref[0:1, :]
    mean = jnp.mean(scaled * value, 1, keepdims=True)
    out = wide(grad_ref[...]) + inverse_rms * scaled - value * (inverse_rms * inverse_rms * inverse_rms * mean)
    out_ref[...] = out
    low_ref[...] = low(out)


def product_kernel(
    section_ref, normed_a, normed_b, grad_a, grad_b, joined_a, joined_b, gate_a, gate_b, mixed_a, mixed_b,
    conv_a, conv_b, head_a, head_b, mix_a, mix_b, skip_a, skip_b, gain_a, gain_b, sent_ref, own_ref,
):
    pl.when(pl.program_id(0) == 0)(
        lambda: fill_products(
            normed_a, normed_b, grad_a, grad_b, joined_a, joined_b, gate_a, gate_b, mixed_a, mixed_b,
            conv_a, conv_b, head_a, head_b, mix_a, mix_b, skip_a, skip_b, gain_a, gain_b, sent_ref,
        )
    )
    pl.when(pl.program_id(0) == 1)(
        lambda: fill_products(
            normed_a, normed_b, grad_a, grad_b, joined_a, joined_b, gate_a, gate_b, mixed_a, mixed_b,
            conv_a, conv_b, head_a, head_b, mix_a, mix_b, skip_a, skip_b, gain_a, gain_b, own_ref,
        )
    )


def fill_products(
    normed_a, normed_b, grad_a, grad_b, joined_a, joined_b, gate_a, gate_b, mixed_a, mixed_b,
    conv_a, conv_b, head_a, head_b, mix_a, mix_b, skip_a, skip_b, gain_a, gain_b, out_ref,
):
    rows = normed_a.shape[1]
    wide_in, inner = joined_a.shape[1], gate_a.shape[1]
    channels = wide_in - LANES
    gate_at, out_at = wide_in, wide_in + inner
    both = lambda left_a, right_a, left_b, right_b: low(
        lead_dot(left_a[...], right_a[...]) + lead_dot(left_b[...], right_b[...])
    )
    out_ref[0:rows, 0:wide_in] = both(normed_a, joined_a, normed_b, joined_b)
    out_ref[0:rows, gate_at:out_at] = both(normed_a, gate_a, normed_b, gate_b)
    out_ref[0:rows, out_at : out_at + inner] = both(grad_a, mixed_a, grad_b, mixed_b)
    pad = lambda value: low(jnp.concatenate([value, jnp.zeros(value.shape, F32)], 0))
    last = slice(rows, rows + 16)
    out_ref[last, 0:channels] = pad(conv_a[...] + conv_b[...])
    out_ref[last, channels:wide_in] = pad(head_a[...] + head_b[...])
    place = iota((8, inner), 0)
    mixes = mix_a[0:1, :] + mix_b[0:1, :]
    skips = skip_a[0:1, :] + skip_b[0:1, :]
    out_ref[last, gate_at:out_at] = pad(jnp.where(place == 0, mixes, jnp.where(place == 1, skips, 0.0)))
    gains = jnp.zeros((8, inner), F32)
    for piece in range(gain_a.shape[1] // inner):
        lanes = slice(piece * inner, (piece + 1) * inner)
        gains = jnp.where(place == piece, gain_a[0:1, lanes] + gain_b[0:1, lanes], gains)
    out_ref[last, out_at : out_at + inner] = pad(gains)


def add_kernel(inner, channels, own_ref, other_ref, keys_ref, across_ref, out_ref):
    step = 48
    for at in range(0, own_ref.shape[0], step):
        rows = slice(at, at + step)
        total = wide(own_ref[rows, :]) + wide(other_ref[rows, :])
        out_ref[rows, :] = low(total)
        keys = wide(keys_ref[rows, :]) + wide(across_ref[rows, :])
        out_ref[rows, inner:channels] = low(total[:, inner:channels] + keys)


def unpack_kernel(inner, keys, section_ref, early_ref, late_ref, other_ref, x_ref, keys_ref, step_ref, gate_ref, out_ref):
    section = section_ref[0]
    mine = pl.program_id(0) == section
    own = jnp.where(section == 0, early_ref[...], late_ref[...])
    value = wide(jnp.where(mine, own, other_ref[...]))
    wide_in = inner + keys + LANES
    x_ref[...] = value[:, :inner]
    keys_ref[...] = value[:, inner : inner + keys]
    step_ref[...] = value[:, inner + keys : wide_in]
    gate_ref[...] = value[:, wide_in : wide_in + inner]
    out_ref[...] = value[:, wide_in + inner :].T


def call(kernel, outs, scratch, micros, *args):
    shapes = [jax.ShapeDtypeStruct(shape, dtype) for shape, dtype in outs]
    moved = sum(a.size * a.dtype.itemsize for a in args) + sum(s.size * s.dtype.itemsize for s in shapes)
    return pl.pallas_call(
        kernel,
        out_shape=shapes,
        in_specs=[pl.BlockSpec(memory_space=pltpu.VMEM)] * len(args),
        out_specs=[pl.BlockSpec(memory_space=pltpu.VMEM)] * len(shapes),
        scratch_shapes=[pltpu.VMEM(shape, dtype) for shape, dtype in scratch],
        compiler_params=pltpu.CompilerParams(vmem_limit_bytes=VMEM),
        cost_estimate=pl.CostEstimate(flops=int(micros * 1.1e9), bytes_accessed=moved, transcendentals=0),
    )(*args)


def pick(halves, index):
    return lax.dynamic_index_in_dim(halves, index, 0, False)


def faded(state, fade):
    per = fade.shape[0]
    rows, lanes = state.shape
    return (state.reshape(per, rows // per, lanes) * fade[:, None, :]).reshape(rows, lanes)


def fade_rows(fade):
    per = fade.shape[0]
    high = wide(low(fade))
    pad = lambda rows: jnp.pad(rows, ((0, 8 - per), (0, 0)))
    return low(jnp.concatenate([pad(high), pad(fade - high)], 0))


def read_fade(rows, per):
    return wide(rows[:per]) + wide(rows[8 : 8 + per])


def scan_states(message, per, fades, reverse):
    blocks = lax.axis_size("seq")
    half = message.shape[1] - (0 if reverse else 16)
    state = message.shape[2]
    if blocks != 8:
        local = message[:, :half].reshape(2 * half, state)
        if fades is None:
            fades = jnp.concatenate([read_fade(message[side, half:], per) for side in range(2)], 0)
        running = jnp.zeros((2 * half, state), F32)
        for _ in range(blocks - 1):
            running = shifted(faded(running, fades) + wide(local), "seq", -1 if reverse else 1)
        return low(running), fades
    side = lax.axis_index("seq") % 2
    even = side == 0
    mine = pick(message, side)
    other = exchange(pick(message, 1 - side), "seq", 1)
    first = jnp.where(even, mine, other)
    second = jnp.where(even, other, mine)
    if fades is None:
        fades = (read_fade(first[half:], per), read_fade(second[half:], per))
    first, second = wide(first[:half]), wide(second[:half])
    fade_first, fade_second = fades
    if reverse:
        total = faded(second, fade_first) + first
    else:
        total = faded(first, fade_second) + second
    sent = jnp.concatenate([low(total), fade_rows(fade_first * fade_second)], 0)
    sign = -1 if reverse else 1
    arrived = [shifted(sent, "seq", sign * 2 * hop) for hop in (1, 2, 3)]
    states = [wide(one[:half]) for one in arrived]
    factors = [read_fade(one[half:], per) for one in arrived]
    entering = states[0] + faded(states[1] + faded(states[2], factors[1]), factors[0])
    if reverse:
        for_second = entering
        for_first = second + faded(entering, fade_second)
    else:
        for_first = entering
        for_second = first + faded(entering, fade_first)
    for_first, for_second = low(for_first), low(for_second)
    kept = jnp.where(even, for_first, for_second)
    back = exchange(jnp.where(even, for_second, for_first), "seq", 1)
    return jnp.concatenate([jnp.where(even, kept, back), jnp.where(even, back, kept)], 0), fades


def layer_forward(entries, normed, weights, next_gain):
    count = len(entries)
    inner = weights["w_z"].shape[1]
    channels = weights["conv"].shape[1]
    features = weights["w_out"].shape[1]
    state = (channels - inner) // 2
    length = entries[0].shape[0]
    heads = 2 * inner // LANES
    joined = [matmul(one, weights["w_in"]) for one in normed]
    before = [shifted(one[length - HALO :, :channels], "seq", 1) for one in joined]
    gate = [matmul(one, weights["w_z"]) for one in normed]
    locals_ = [
        call(
            local_kernel,
            [
                ((length, inner), F32),
                ((2, inner // 2 + 16, state), BF16),
                ((length, state), BF16),
                ((length, LANES), F32),
            ],
            [((HALO + length, channels), F32), ((length, channels), F32)],
            3.2,
            joined[index], before[index], weights["conv"], weights["head"],
        )
        for index in range(count)
    ]
    scans = [scan_states(one[1], heads // 2, None, False) for one in locals_]
    finished = [
        call(
            output_kernel,
            [((length, inner), F32), ((length, features + LANES), BF16)],
            [((length, inner), BF16)],
            2.5,
            one[0], one[2], one[3], scan[0], gate[index], weights["mix"], weights["w_out"],
        )
        for index, (one, scan) in enumerate(zip(locals_, scans))
    ]
    outputs = []
    next_normed = []
    kept = []
    total_inner = inner * lax.axis_size("head")
    for index in range(count):
        ssd_out, part = finished[index]
        bit = 1
        while 2 * bit < lax.axis_size("head"):
            total = wide(part) + wide(exchange(part, "head", bit))
            squares = jnp.sum(total[:, features:], 1, keepdims=True)
            high = wide(low(squares))
            tail = jnp.pad(jnp.concatenate([high, squares - high], 1), ((0, 0), (0, LANES - 2)))
            part = low(jnp.concatenate([total[:, :features], tail], 1))
            bit *= 2
        out, branch, scale, later = call(
            functools.partial(merge_kernel, total_inner),
            [
                ((length, features), BF16),
                ((length, features), F32),
                ((length, LANES), F32),
                ((length, features), BF16),
            ],
            [],
            1.0,
            part, exchange(part, "head", bit), entries[index], next_gain,
        )
        outputs.append(out)
        next_normed.append(later)
        kept.append(
            dict(
                entry=entries[index], normed=normed[index],
                joined=joined[index], before=before[index], gate=gate[index],
                read=locals_[index][2], rise=locals_[index][3], start=scans[index][0],
                fades=scans[index][1], ssd_out=ssd_out, scale=scale, branch=branch,
            )
        )
    return outputs, next_normed, kept


def layer_backward(grads, lows, kept, weights):
    count = len(grads)
    inner = weights["w_z"].shape[1]
    channels = weights["conv"].shape[1]
    features = weights["w_out"].shape[1]
    state = (channels - inner) // 2
    length = grads[0].shape[0]
    heads = 2 * inner // LANES
    total_inner = inner * lax.axis_size("head")
    gates = []
    for grad_low, one in zip(lows, kept):
        gates.append(
            call(
                functools.partial(gate_back_kernel, total_inner),
                [
                    ((length, inner), F32),
                    ((length, inner), BF16),
                    ((length, inner), BF16),
                    ((2, inner // 2, state), BF16),
                    ((8, inner), F32),
                ],
                [],
                3.9,
                grad_low, weights["w_out"], one["ssd_out"], one["gate"], one["scale"],
                one["branch"], weights["mix"], one["rise"], one["read"],
            )
        )
    scans = [scan_states(gate[3], heads // 2, one["fades"], True)[0] for gate, one in zip(gates, kept)]
    mixes = [
        call(
            scan_back_kernel,
            [
                ((length, inner), F32),
                ((length, 2 * state), F32),
                ((length, 2 * LANES), F32),
                ((8, inner), F32),
            ],
            [
                ((HALO + length, channels), F32),
                ((length, channels), F32),
                ((LANES, length), F32),
                ((length, length), F32),
                ((length, inner), F32),
            ],
            6.8,
            one["joined"], one["before"], weights["conv"], weights["head"], gate[0], one["start"],
        )
        for gate, one in zip(gates, kept)
    ]
    states = [
        call(
            state_back_kernel,
            [
                ((length, channels), F32),
                ((length, LANES), BF16),
                ((8, channels), F32),
                ((8, LANES), F32),
            ],
            [((HALO + length, channels), F32), ((length, inner), F32)],
            4.1,
            one["joined"], one["before"], weights["conv"], weights["head"],
            mix[0], mix[1], mix[2], scan, one["start"],
        )
        for mix, scan, one in zip(mixes, scans, kept)
    ]
    after = [shifted(one[0][:HALO], "seq", -1) for one in states]
    inputs = [
        call(
            input_back_kernel,
            [((length, channels + LANES), BF16), ((length, features), BF16)],
            [((length + HALO, channels), F32)],
            2.0,
            one[0], rim, weights["conv"], one[1], gate[1], weights["w_in"], weights["w_z"],
        )
        for one, rim, gate in zip(states, after, gates)
    ]
    results = []
    for index in range(count):
        one = kept[index]
        part = inputs[index][1]
        bit = 1
        while 2 * bit < lax.axis_size("head"):
            part = low(wide(part) + wide(exchange(part, "head", bit)))
            bit *= 2
        results.append(
            call(
                entry_back_kernel,
                [((length, features), F32), ((length, features), BF16), ((8, features), F32)],
                [],
                1.2,
                part, exchange(part, "head", bit), one["entry"], weights["gain"], grads[index],
            )
        )
    pairs = (
        [one["normed"] for one in kept], lows, [one[0] for one in inputs], [one[1] for one in gates],
        [one[2] for one in gates], [one[2] for one in states], [one[3] for one in states],
        [one[4] for one in gates], [one[3] for one in mixes], [one[2] for one in results],
    )
    return results, reduced(pairs, inner, channels)


NAMES = (
    "norm_gain", "w_z", "w_x", "w_bc", "w_dt", "dt_bias", "a_log", "d_skip",
    "conv_x", "conv_bias_x", "conv_bc", "conv_bias_bc", "mix_gain", "w_out",
)


def packed(mine):
    inner = mine["w_z"].shape[1]
    lanes = lambda rows, width: jnp.pad(rows, ((0, 0), (0, width - rows.shape[1])))
    heads = mine["w_dt"].shape[1]
    w_in = jnp.concatenate([mine["w_x"], mine["w_bc"], lanes(mine["w_dt"], LANES)], 1)
    keys = mine["w_bc"].shape[1]
    bias = jnp.concatenate([mine["conv_bias_x"], mine["conv_bias_bc"]], 0)[None]
    skip = lanes(jnp.repeat(mine["d_skip"], inner // heads)[None], inner + keys)
    conv = jnp.concatenate([mine["conv_x"], mine["conv_bc"]], 1)
    rows = jnp.concatenate([conv, bias, skip, jnp.zeros((2, inner + keys), F32)], 0)
    head = lanes(jnp.stack([mine["dt_bias"], mine["a_log"]]), LANES)
    vectors = jnp.concatenate([lanes(head, LANES), jnp.zeros((6, LANES), F32)], 0)
    mix = jnp.pad(mine["mix_gain"][None], ((0, 7), (0, 0)))
    gain = jnp.pad(mine["norm_gain"][None], ((0, 7), (0, 0)))
    return dict(w_in=w_in, w_z=mine["w_z"], w_out=mine["w_out"], small=jnp.concatenate([rows, vectors, mix, gain], 1))


def both_layers(mine):
    first = lax.axis_index("section") == 0
    inner = mine["w_z"].shape[1]
    channels = inner + mine["w_bc"].shape[1]
    own = packed(mine)
    other = {name: exchange(own[name], "section", 1) for name in ("small", "w_in")}
    own["w_z"], own["w_out"], other["w_in"] = lax.optimization_barrier(
        (own["w_z"], own["w_out"], other["w_in"])
    )
    other.update({name: exchange(own[name], "section", 1) for name in ("w_z", "w_out")})

    def layer(flag):
        chosen = {name: jnp.where(flag, own[name], other[name]) for name in own}
        small = chosen.pop("small")
        chosen["conv"] = small[:, :channels]
        chosen["head"] = small[:, channels : channels + LANES]
        chosen["mix"] = small[:, channels + LANES : channels + LANES + inner]
        chosen["gain"] = small[:, channels + LANES + inner :]
        return chosen

    return layer(first), layer(~first)


def reduced(pairs, inner, channels):
    section = lax.axis_index("section")
    length, features = pairs[0][0].shape
    half = features // 2
    width = channels + LANES + 2 * inner
    whole = lambda array: pl.BlockSpec(array.shape, lambda i, side: (0, 0))
    split = pl.BlockSpec((length, half), lambda i, side: (0, (1 - side[0]) * (1 - i) + side[0] * i))
    flat = [array for pair in pairs for array in pair]
    given = pl.BlockSpec((half + 16, width), lambda i, side: (0, 0))
    shape = jax.ShapeDtypeStruct((half + 16, width), BF16)
    sent, own = pl.pallas_call(
        product_kernel,
        grid_spec=pltpu.PrefetchScalarGridSpec(
            num_scalar_prefetch=1,
            grid=(2,),
            in_specs=[split] * 4 + [whole(array) for array in flat[4:]],
            out_specs=[given, given],
        ),
        out_shape=[shape, shape],
        compiler_params=pltpu.CompilerParams(vmem_limit_bytes=2 * VMEM),
        cost_estimate=pl.CostEstimate(flops=8 * 10**9, bytes_accessed=1 << 24, transcendentals=0),
    )(jnp.full((1,), section, jnp.int32), *flat)
    other = exchange(sent, "section", 1)
    heads = lax.axis_size("head")
    if heads == 2:
        keys = exchange(own[:, inner:channels], "head", 1)
        route = [(i, i ^ 3) for i in range(4)]
        across = lax.ppermute(sent[:, inner:channels], ("section", "head"), route)
    else:
        mine = wide(own[:, inner:channels]) + wide(other[:, inner:channels])
        keys = low(head_sum(mine) - mine)
        across = jnp.zeros_like(keys)
    return call(
        functools.partial(add_kernel, inner, channels), [(own.shape, BF16)], [], 4.0, own, other, keys, across
    )[0]


def shards(hidden_in, order, cotangent, *params):
    mine = {name: param[0] for name, param in zip(NAMES, params)}
    layers = both_layers(mine)
    sections = lax.axis_size("section")
    section = lax.axis_index("section")
    first = section == 0
    count = order.shape[0] // sections
    base = section * count
    inner = mine["w_z"].shape[1]
    channels = inner + mine["w_bc"].shape[1]
    features = hidden_in.shape[2]
    entries = [pick(hidden_in, order[base + index]) for index in range(count)]
    gains = [weights["gain"] for weights in layers]
    normed = [normalized(wide(entry), gains[0][0:1]) for entry in entries]
    outputs = []
    kept = []
    for index, weights in enumerate(layers):
        entries, normed, one = layer_forward(entries, normed, weights, gains[1])
        outputs.append(jnp.stack(entries))
        kept.append(one)
    incoming = [pick(cotangent, base + index) for index in range(count)]
    results, late = layer_backward(incoming, incoming, kept[1], layers[1])
    late_grads = jnp.stack([one[0] for one in results])
    wides = [one[0] for one in results]
    lows = [one[1] for one in results]
    results, early = layer_backward(lows, lows, kept[0], layers[0])
    early_grads = jnp.stack([one[0] for one in results])
    early, late = lax.psum((early, late), "seq")

    def swapped(early, late):
        return exchange(jnp.where(first, late, early), "section", 1)

    def to_owner(early, late):
        own, sent = jnp.where(first, early, late), swapped(early, late)
        return jnp.concatenate([jnp.where(first, own, sent), jnp.where(first, sent, own)], 0)

    activations = to_owner(outputs[0], outputs[1])[None]
    grads = to_owner(early_grads, late_grads)[None]
    half = features // 2
    keys_width = channels - inner
    early, late, activations, grads = lax.optimization_barrier((early, late, activations, grads))
    other = swapped(early, late)
    block = 128
    steps = half // block
    width = early.shape[1]
    taken = pl.BlockSpec((block, width), lambda side, i: (i, 0))
    given = lambda lanes: pl.BlockSpec((block, lanes), lambda side, i: (side * steps + i, 0))
    shape = lambda rows, lanes: jax.ShapeDtypeStruct((rows, lanes), F32)
    w_x, w_bc, w_dt, w_z, w_out = pl.pallas_call(
        functools.partial(unpack_kernel, inner, keys_width),
        grid=(2, steps),
        out_shape=[
            shape(features, inner), shape(features, keys_width), shape(features, LANES),
            shape(features, inner), shape(inner, features),
        ],
        in_specs=[pl.BlockSpec(memory_space=pltpu.SMEM), taken, taken, taken],
        out_specs=[
            given(inner), given(keys_width), given(LANES), given(inner),
            pl.BlockSpec((inner, block), lambda side, i: (0, side * steps + i)),
        ],
        compiler_params=pltpu.CompilerParams(vmem_limit_bytes=VMEM),
    )(jnp.full((1,), section, jnp.int32), early, late, other)
    rows = wide(jnp.where(first, early[half : half + 8], late[half : half + 8]))
    heads = mine["w_dt"].shape[1]
    wide_in = channels + LANES
    mixes = rows[:, wide_in : wide_in + inner]
    gains = rows[: features // inner, wide_in + inner :].reshape(features)
    results = dict(
        norm_gain=gains,
        w_z=w_z,
        w_x=w_x,
        w_bc=w_bc,
        w_dt=w_dt[:, :heads],
        dt_bias=rows[0, channels : channels + heads],
        a_log=rows[1, channels : channels + heads],
        d_skip=jnp.sum(mixes[1].reshape(heads, -1), 1),
        conv_x=rows[:4, :inner],
        conv_bias_x=rows[4, :inner],
        conv_bc=rows[:4, inner:channels],
        conv_bias_bc=rows[4, inner:channels],
        mix_gain=mixes[0],
        w_out=w_out,
    )
    return (activations, grads) + tuple(results[name][None] for name in NAMES)


def solution(mesh):
    in_specs = (
        P(None, "seq", None),
        P(),
        P(None, "seq", None),
        P("section", None),
        P("section", None, "head"),
        P("section", None, "head"),
        P("section", None, None),
        P("section", None, "head"),
        P("section", "head"),
        P("section", "head"),
        P("section", "head"),
        P("section", None, "head"),
        P("section", "head"),
        P("section", None, None),
        P("section", None),
        P("section", "head"),
        P("section", "head", None),
    )
    out_specs = (
        P("section", None, "seq", None),
        P("section", None, "seq", None),
        P("section", None),
        P("section", None, "head"),
        P("section", None, "head"),
        P("section", None, None),
        P("section", None, "head"),
        P("section", "head"),
        P("section", "head"),
        P("section", "head"),
        P("section", None, "head"),
        P("section", "head"),
        P("section", None, None),
        P("section", None),
        P("section", "head"),
        P("section", "head", None),
    )
    return jax.shard_map(shards, mesh=mesh, in_specs=in_specs, out_specs=out_specs, check_vma=False)
```

```python
import functools

import jax
import jax.numpy as jnp
from jax import lax
from jax.experimental import pallas as pl
from jax.experimental.pallas import tpu as pltpu
from jax.sharding import PartitionSpec as P

EPS = 1e-05
F32 = jnp.float32
BF16 = jnp.bfloat16
LANES = 128
HALO = 8
VMEM = 24 * 1024 * 1024


def exchange(block, axis, bit):
    route = [(i, i ^ bit) for i in range(lax.axis_size(axis))]
    return lax.ppermute(block, axis, route)


def shifted(block, axis, distance):
    devices = range(lax.axis_size(axis))
    route = [(i - distance, i) for i in devices if i - distance in devices]
    return lax.ppermute(block, axis, route)


def low(value):
    return value.astype(BF16)


def wide(value):
    return value.astype(F32)


def matmul(left, right):
    return jnp.dot(left, right, preferred_element_type=F32)


def lead_dot(left, right):
    return lax.dot_general(left, right, (((0,), (0,)), ((), ())), preferred_element_type=F32)


def tail_dot(left, right):
    return lax.dot_general(left, right, (((1,), (1,)), ((), ())), preferred_element_type=F32)


def head_sum(part):
    bit = 1
    while bit < lax.axis_size("head"):
        part = low(part)
        part = wide(part) + wide(exchange(part, "head", bit))
        bit *= 2
    return part


def parts_of(value, count):
    terms = []
    for _ in range(count):
        term = low(value)
        terms.append(term)
        value = value - wide(term)
    return terms


def dot_parts(left, right, count, dot=matmul):
    return sum(dot(left, term) for term in parts_of(right, count))


def iota(shape, axis):
    return lax.broadcasted_iota(jnp.int32, shape, axis)


def lower_mask(length):
    return iota((length, length), 0) >= iota((length, length), 1)


def expand(values, pair):
    length = values.shape[0]
    early = iota((length, LANES), 1) < LANES // 2
    first = values[:, 2 * pair : 2 * pair + 1]
    second = values[:, 2 * pair + 1 : 2 * pair + 2]
    return jnp.where(early, first, second)


def head_matrix(inner, width):
    return jnp.where(iota((inner, LANES), 0) // width == iota((inner, LANES), 1), 1.0, 0.0).astype(BF16)


def head_sums(values, matrix):
    high, rest = parts_of(values, 2)
    return matmul(high, matrix) + matmul(rest, matrix)


def sigmoid(value):
    return 1.0 / (1.0 + jnp.exp(-value))


def softplus(value):
    tail = jnp.exp(-jnp.abs(value))
    shifted_one = 1.0 + tail
    gap = shifted_one - 1.0
    small = jnp.where(gap == 0.0, tail, jnp.log(shifted_one) * (tail / jnp.where(gap == 0.0, 1.0, gap)))
    return jnp.maximum(value, 0.0) + small


def conv_preact(joined_ref, before_ref, conv_ref, ext_ref):
    length, channels = joined_ref.shape[0], conv_ref.shape[1]
    ext_ref[0:HALO, :] = before_ref[...]
    ext_ref[HALO : HALO + length, :] = joined_ref[:, 0:channels]
    total = conv_ref[4:5, :]
    for tap in range(4):
        total = total + conv_ref[tap : tap + 1, :] * ext_ref[HALO - 3 + tap : HALO - 3 + tap + length, :]
    return total


def decays(joined_ref, head_ref, channels):
    length = joined_ref.shape[0]
    raw = joined_ref[:, channels : channels + LANES] + head_ref[0:1, :]
    step = softplus(raw)
    rate = -jnp.exp(head_ref[1:2, :])
    lower = jnp.where(lower_mask(length), 1.0, 0.0).astype(BF16)
    decay_sum = dot_parts(lower, rate * step, 3)
    return raw, step, rate, decay_sum


def pair_dots(early, mixing_a, mixing_b, values, dot):
    return jnp.where(early, dot(mixing_a, values), dot(mixing_b, values))


def local_kernel(joined_ref, before_ref, conv_ref, head_ref, y_ref, message_ref, read_ref, rise_ref, ext_ref, act_ref):
    length = joined_ref.shape[0]
    channels = conv_ref.shape[1]
    inner = y_ref.shape[1]
    state = read_ref.shape[1]
    pairs = inner // LANES
    preact = conv_preact(joined_ref, before_ref, conv_ref, ext_ref)
    act_ref[...] = preact * sigmoid(preact)
    write_low = low(act_ref[:, inner : inner + state])
    read_low = low(act_ref[:, inner + state : inner + 2 * state])
    read_ref[...] = read_low
    _, step, _, decay_sum = decays(joined_ref, head_ref, channels)
    rise_ref[...] = jnp.exp(decay_sum)
    keep_step = jnp.exp(decay_sum[length - 1 : length, :] - decay_sum) * step
    decay_rows = decay_sum.T
    step_rows = step.T
    gram = tail_dot(read_low, write_low)
    lower = lower_mask(length)
    early = iota((length, LANES), 1) < LANES // 2
    half = inner // 2
    for pair in range(pairs):
        lanes = slice(pair * LANES, (pair + 1) * LANES)
        signal = act_ref[:, lanes]
        signal_low = low(signal)
        mixings = []
        for head in (2 * pair, 2 * pair + 1):
            diff = decay_sum[:, head : head + 1] - decay_rows[head : head + 1, :]
            decay = jnp.exp(jnp.where(lower, diff, -1e30))
            mixings.append(low(gram * decay * step_rows[head : head + 1, :]))
        mixed = pair_dots(early, mixings[0], mixings[1], signal_low, matmul)
        y_ref[:, lanes] = mixed + conv_ref[5:6, lanes] * signal
        local = lead_dot(low(expand(keep_step, pair) * signal), write_low)
        place = pair * LANES
        if half % LANES == 0:
            side, row = place // half, place % half
            message_ref[side, row : row + LANES, :] = low(local)
    heads = 2 * pairs
    per = heads // 2
    for side in range(2):
        column = jnp.exp(decay_rows[side * per : side * per + 8, length - 1 : length])
        fade = jnp.broadcast_to(column, (8, state))
        high = wide(low(fade))
        message_ref[side, half : half + 16, :] = low(jnp.concatenate([high, fade - high], 0))


def output_kernel(y_ref, read_ref, rise_ref, start_ref, gate_ref, mix_ref, w_ref, ssd_ref, part_ref, mixed_ref):
    length, inner = y_ref.shape
    features = w_ref.shape[1]
    squares = jnp.zeros((length, 1), F32)
    for pair in range(inner // LANES):
        lanes = slice(pair * LANES, (pair + 1) * LANES)
        reach = tail_dot(read_ref[...], start_ref[lanes, :])
        ssd_out = y_ref[:, lanes] + expand(rise_ref[...], pair) * reach
        ssd_ref[:, lanes] = ssd_out
        gate = gate_ref[:, lanes]
        gated = ssd_out * (gate * sigmoid(gate))
        squares = squares + jnp.sum(gated * gated, 1, keepdims=True)
        mixed_ref[:, lanes] = low(gated * mix_ref[0:1, lanes])
    part_ref[:, 0:features] = low(matmul(mixed_ref[...], w_ref[...]))
    high = wide(low(squares))
    lane = iota((length, LANES), 1)
    tail = jnp.where(lane == 0, high, jnp.where(lane == 1, squares - high, 0.0))
    part_ref[:, features : features + LANES] = low(tail)


def gate_back_kernel(
    total_inner, grad_ref, w_ref, ssd_ref, gate_ref, scale_ref, branch_ref, mix_ref, rise_ref, read_ref,
    grad_y_ref, gate_low_ref, mixed_ref, start_ref, sums_ref,
):
    length, inner = ssd_ref.shape
    scale = scale_ref[:, 0:1]
    along = jnp.sum(wide(grad_ref[...]) * branch_ref[...], 1, keepdims=True) * (scale * scale / total_inner)
    half = inner // 2
    sums_ref[...] = jnp.zeros(sums_ref.shape, F32)
    for pair in range(inner // LANES):
        lanes = slice(pair * LANES, (pair + 1) * LANES)
        grad_mixed = tail_dot(grad_ref[...], w_ref[lanes, :])
        gain = mix_ref[0:1, lanes]
        gate = gate_ref[:, lanes]
        ssd_out = ssd_ref[:, lanes]
        sigma = sigmoid(gate)
        active = gate * sigma
        gated = ssd_out * active
        normal = gated * scale
        sums_ref[0:1, lanes] = jnp.sum(grad_mixed * normal, 0, keepdims=True)
        mixed_ref[:, lanes] = low(normal * gain)
        grad_gated = scale * (grad_mixed * gain) - gated * along
        grad_y = grad_gated * active
        grad_y_ref[:, lanes] = grad_y
        gate_low_ref[:, lanes] = low(grad_gated * ssd_out * (sigma * (1.0 + gate * (1.0 - sigma))))
        grad_reach = low(grad_y * expand(rise_ref[...], pair))
        grad_start = lead_dot(grad_reach, read_ref[...])
        place = pair * LANES
        if half % LANES == 0:
            side, row = place // half, place % half
            start_ref[side, row : row + LANES, :] = low(grad_start)


def scan_back_kernel(
    joined_ref, before_ref, conv_ref, head_ref, grad_y_ref, start_ref,
    signal_ref, keys_ref, sums_ref, row_ref,
    ext_ref, act_ref, step_ref, gram_ref, prod_ref,
):
    length, inner = grad_y_ref.shape
    channels = conv_ref.shape[1]
    state = start_ref.shape[1]
    pairs = inner // LANES
    preact = conv_preact(joined_ref, before_ref, conv_ref, ext_ref)
    act_ref[...] = preact * sigmoid(preact)
    write_low = low(act_ref[:, inner : inner + state])
    read_low = low(act_ref[:, inner + state : inner + 2 * state])
    _, step, _, decay_sum = decays(joined_ref, head_ref, channels)
    rise = jnp.exp(decay_sum)
    decay_rows = decay_sum.T
    step_rows = step.T
    gram = tail_dot(read_low, write_low)
    lower = lower_mask(length)
    early = iota((length, LANES), 1) < LANES // 2
    lane = iota((length, LANES), 1)
    step_ref[...] = jnp.zeros(step_ref.shape, F32)
    gram_ref[...] = jnp.zeros(gram_ref.shape, F32)
    columns = jnp.zeros((length, LANES), F32)
    grad_read = jnp.zeros((length, state), F32)
    row_ref[...] = jnp.zeros(row_ref.shape, F32)
    for pair in range(pairs):
        lanes = slice(pair * LANES, (pair + 1) * LANES)
        signal = act_ref[:, lanes]
        signal_low = low(signal)
        grad_y = grad_y_ref[:, lanes]
        grad_y_low = low(grad_y)
        mixings = []
        for head in (2 * pair, 2 * pair + 1):
            mine = early if head % 2 == 0 else jnp.logical_not(early)
            own = jnp.where(mine, grad_y, 0.0)
            grad_mixing = tail_dot(low(own), signal_low)
            diff = decay_sum[:, head : head + 1] - decay_rows[head : head + 1, :]
            decay = jnp.exp(jnp.where(lower, diff, -1e30))
            step_row = step_rows[head : head + 1, :]
            plain = gram * decay
            mixings.append(low(plain * step_row))
            gram_ref[...] += grad_mixing * decay * step_row
            weighed = grad_mixing * plain
            step_ref[head : head + 1, :] = jnp.sum(weighed, 0, keepdims=True)
            columns = jnp.where(lane == head, jnp.sum(weighed * step_row, 1, keepdims=True), columns)
        back = pair_dots(early, mixings[0], mixings[1], grad_y_low, lead_dot)
        signal_ref[:, lanes] = conv_ref[5:6, lanes] * grad_y + back
        row_ref[0:1, lanes] = jnp.sum(grad_y * signal, 0, keepdims=True)
        start = start_ref[lanes, :]
        reach = tail_dot(read_low, start)
        prod_ref[:, lanes] = grad_y * reach
        grad_read = grad_read + matmul(low(grad_y * expand(rise, pair)), start)
    gram_parts = parts_of(gram_ref[...], 2)
    keys_ref[:, 0:state] = sum(lead_dot(part, read_low) for part in gram_parts)
    keys_ref[:, state : 2 * state] = grad_read + sum(matmul(part, write_low) for part in gram_parts)
    grad_step = step_ref[...].T
    matrix = head_matrix(inner, LANES // 2)
    sums_ref[:, 0:LANES] = columns - step * grad_step + head_sums(prod_ref[...], matrix) * rise
    sums_ref[:, LANES : 2 * LANES] = grad_step


def state_back_kernel(
    joined_ref, before_ref, conv_ref, head_ref, signal_ref, keys_ref, sums_ref, local_ref, start_ref,
    pre_ref, raw_ref, conv_sums_ref, head_sums_ref,
    ext_ref, prod_ref,
):
    length, inner = signal_ref.shape
    channels = conv_ref.shape[1]
    state = start_ref.shape[1]
    preact = conv_preact(joined_ref, before_ref, conv_ref, ext_ref)
    raw, step, rate, decay_sum = decays(joined_ref, head_ref, channels)
    keep = jnp.exp(decay_sum[length - 1 : length, :] - decay_sum)
    tail = keep * step
    sigma = sigmoid(preact)
    active = preact * sigma
    slope = sigma * (1.0 + preact * (1.0 - sigma))
    write_low = low(active[:, inner : inner + state])
    grad_write = keys_ref[:, 0:state]
    conv_sums_ref[...] = jnp.zeros(conv_sums_ref.shape, F32)

    def finish(grad, lanes):
        grad_pre = grad * slope[:, lanes]
        pre_ref[:, lanes] = grad_pre
        for tap in range(4):
            rows = ext_ref[HALO - 3 + tap : HALO - 3 + tap + length, lanes]
            conv_sums_ref[tap : tap + 1, lanes] = jnp.sum(grad_pre * rows, 0, keepdims=True)
        conv_sums_ref[4:5, lanes] = jnp.sum(grad_pre, 0, keepdims=True)

    for pair in range(inner // LANES):
        lanes = slice(pair * LANES, (pair + 1) * LANES)
        signal = active[:, lanes]
        local = local_ref[lanes, :]
        spread = tail_dot(write_low, local)
        wide_tail = expand(tail, pair)
        prod_ref[:, lanes] = signal * spread
        grad_write = grad_write + matmul(low(wide_tail * signal), local)
        finish(signal_ref[:, lanes] + wide_tail * spread, lanes)
    finish(grad_write, slice(inner, inner + state))
    finish(keys_ref[:, state : 2 * state], slice(inner + state, inner + 2 * state))
    matrix = head_matrix(inner, LANES // 2)
    grad_tail = head_sums(prod_ref[...], matrix)
    grad_step = sums_ref[:, LANES : 2 * LANES] + grad_tail * keep
    tail_log = grad_tail * tail
    product = wide(local_ref[...]) * wide(start_ref[...])
    by_state = sum(lead_dot(matrix, part) for part in parts_of(product, 2))
    ones = jnp.ones((8, state), BF16)
    totals = sum(tail_dot(ones, part) for part in parts_of(by_state, 2))[0:1, :]
    fade = jnp.exp(decay_sum[length - 1 : length, :])
    last = iota((length, LANES), 0) == length - 1
    extra = jnp.sum(tail_log, 0, keepdims=True) + totals * fade
    grad_decay = sums_ref[:, 0:LANES] - tail_log + jnp.where(last, extra, 0.0)
    upper = jnp.where(iota((length, length), 1) >= iota((length, length), 0), 1.0, 0.0).astype(BF16)
    grad_log = dot_parts(upper, grad_decay, 3)
    grad_step = grad_step + grad_log * rate
    grad_raw = grad_step * sigmoid(raw)
    raw_ref[...] = low(grad_raw)
    head_sums_ref[...] = jnp.zeros(head_sums_ref.shape, F32)
    head_sums_ref[0:1, :] = jnp.sum(grad_raw, 0, keepdims=True)
    head_sums_ref[1:2, :] = jnp.sum(grad_log * step, 0, keepdims=True) * rate


def input_back_kernel(pre_ref, after_ref, conv_ref, raw_ref, gate_ref, w_ref, w_gate_ref, joined_ref, part_ref, ext_ref):
    length, channels = pre_ref.shape
    ext_ref[0:length, :] = pre_ref[...]
    ext_ref[length : length + HALO, :] = after_ref[...]
    total = jnp.zeros((length, channels), F32)
    for tap in range(4):
        total = total + conv_ref[tap : tap + 1, :] * ext_ref[3 - tap : 3 - tap + length, :]
    joined_ref[:, 0:channels] = low(total)
    joined_ref[:, channels : channels + LANES] = raw_ref[...]
    part_ref[...] = low(tail_dot(joined_ref[...], w_ref[...]) + tail_dot(gate_ref[...], w_gate_ref[...]))


def normalized(value, gain):
    return low(value * lax.rsqrt(jnp.mean(value * value, 1, keepdims=True) + EPS) * gain)


def merge_kernel(total_inner, part_ref, other_ref, entry_ref, gain_ref, out_ref, branch_ref, scale_ref, normed_ref):
    features = entry_ref.shape[1]
    total = wide(part_ref[...]) + wide(other_ref[...])
    squares = jnp.sum(total[:, features:], 1, keepdims=True)
    scale = lax.rsqrt(squares / total_inner + EPS)
    branch = scale * total[:, :features]
    out = low(wide(entry_ref[...]) + branch)
    out_ref[...] = out
    branch_ref[...] = branch
    scale_ref[...] = jnp.broadcast_to(scale, scale_ref.shape)
    normed_ref[...] = normalized(wide(out), gain_ref[0:1, :])


def entry_back_kernel(part_ref, other_ref, entry_ref, gain_ref, grad_ref, out_ref, low_ref, sums_ref):
    grad_normed = wide(part_ref[...]) + wide(other_ref[...])
    value = wide(entry_ref[...])
    inverse_rms = lax.rsqrt(jnp.mean(value * value, 1, keepdims=True) + EPS)
    sums_ref[...] = jnp.zeros(sums_ref.shape, F32)
    sums_ref[0:1, :] = jnp.sum(grad_normed * value * inverse_rms, 0, keepdims=True)
    scaled = grad_normed * gain_ref[0:1, :]
    mean = jnp.mean(scaled * value, 1, keepdims=True)
    out = wide(grad_ref[...]) + inverse_rms * scaled - value * (inverse_rms * inverse_rms * inverse_rms * mean)
    out_ref[...] = out
    low_ref[...] = low(out)


def product_kernel(
    half_ref, normed_a, normed_b, grad_a, grad_b, joined_a, joined_b, gate_a, gate_b, mixed_a, mixed_b,
    conv_a, conv_b, head_a, head_b, mix_a, mix_b, skip_a, skip_b, out_ref,
):
    rows = normed_a.shape[1]
    wide_in, inner = joined_a.shape[1], gate_a.shape[1]
    channels = wide_in - LANES
    gate_at, out_at = wide_in, wide_in + inner
    both = lambda left_a, right_a, left_b, right_b: low(
        lead_dot(left_a[...], right_a[...]) + lead_dot(left_b[...], right_b[...])
    )
    out_ref[0:rows, 0:wide_in] = both(normed_a, joined_a, normed_b, joined_b)
    out_ref[0:rows, gate_at:out_at] = both(normed_a, gate_a, normed_b, gate_b)
    out_ref[0:rows, out_at : out_at + inner] = both(grad_a, mixed_a, grad_b, mixed_b)
    pad = lambda value: low(jnp.concatenate([value, jnp.zeros(value.shape, F32)], 0))
    last = slice(rows, rows + 16)
    out_ref[last, 0:channels] = pad(conv_a[...] + conv_b[...])
    out_ref[last, channels:wide_in] = pad(head_a[...] + head_b[...])
    place = iota((8, inner), 0)
    mixes = mix_a[0:1, :] + mix_b[0:1, :]
    skips = skip_a[0:1, :] + skip_b[0:1, :]
    out_ref[last, gate_at:out_at] = pad(jnp.where(place == 0, mixes, jnp.where(place == 1, skips, 0.0)))
    out_ref[last, out_at : out_at + inner] = jnp.zeros((16, inner), BF16)


def add_kernel(inner, channels, own_ref, other_ref, keys_ref, across_ref, gains_ref, out_ref, rest_ref):
    step = 48
    half, cut = own_ref.shape[0] - 16, out_ref.shape[1]
    for at in range(0, own_ref.shape[0], step):
        rows = slice(at, at + step)
        total = wide(own_ref[rows, :]) + wide(other_ref[rows, :])
        out_ref[rows, :] = low(total[:, :cut])
        rest_ref[rows, :] = low(total[:, cut:])
        keys = wide(keys_ref[rows, :]) + wide(across_ref[rows, :])
        out_ref[rows, inner:channels] = low(total[:, inner:channels] + keys)
    rest_ref[half : half + 16, :] = low(gains_ref[...])


def unpack_kernel(inner, keys, section_ref, early_ref, early_rest_ref, late_ref, late_rest_ref, *refs):
    x_ref, keys_ref, step_ref, gate_ref, out_ref = refs[-5:]
    value = wide(jnp.where(section_ref[0] == 0, early_ref[...], late_ref[...]))
    wide_in = inner + keys + LANES
    x_ref[...] = value[:, :inner]
    keys_ref[...] = value[:, inner : inner + keys]
    step_ref[...] = value[:, inner + keys : wide_in]
    gate_ref[...] = value[:, wide_in : wide_in + inner]
    rest = jnp.where(section_ref[0] == 0, early_rest_ref[...], late_rest_ref[...])
    out_ref[...] = wide(rest).T


def call(kernel, outs, scratch, micros, *args):
    shapes = [jax.ShapeDtypeStruct(shape, dtype) for shape, dtype in outs]
    moved = sum(a.size * a.dtype.itemsize for a in args) + sum(s.size * s.dtype.itemsize for s in shapes)
    return pl.pallas_call(
        kernel,
        out_shape=shapes,
        in_specs=[pl.BlockSpec(memory_space=pltpu.VMEM)] * len(args),
        out_specs=[pl.BlockSpec(memory_space=pltpu.VMEM)] * len(shapes),
        scratch_shapes=[pltpu.VMEM(shape, dtype) for shape, dtype in scratch],
        compiler_params=pltpu.CompilerParams(vmem_limit_bytes=VMEM),
        cost_estimate=pl.CostEstimate(flops=int(micros * 1.1e9), bytes_accessed=moved, transcendentals=0),
    )(*args)


def pick(halves, index):
    return lax.dynamic_index_in_dim(halves, index, 0, False)


def faded(state, fade):
    per = fade.shape[0]
    rows, lanes = state.shape
    return (state.reshape(per, rows // per, lanes) * fade[:, None, :]).reshape(rows, lanes)


def fade_rows(fade):
    per = fade.shape[0]
    high = wide(low(fade))
    pad = lambda rows: jnp.pad(rows, ((0, 8 - per), (0, 0)))
    return low(jnp.concatenate([pad(high), pad(fade - high)], 0))


def read_fade(rows, per):
    return wide(rows[:per]) + wide(rows[8 : 8 + per])


def tree_sum(part):
    me = lax.axis_index("seq")
    bit = 1
    while bit < lax.axis_size("seq"):
        half = part.shape[1] // 2
        upper = (me & bit) != 0
        left, right = part[:, :half], part[:, half:]
        sent = jnp.where(upper, left, right)
        part = low(wide(jnp.where(upper, right, left)) + wide(exchange(sent, "seq", bit)))
        bit *= 2
    while bit > 1:
        bit //= 2
        upper = (me & bit) != 0
        other = exchange(part, "seq", bit)
        part = jnp.concatenate([jnp.where(upper, other, part), jnp.where(upper, part, other)], 1)
    return part


def scan_states(message, per, fades, reverse):
    blocks = lax.axis_size("seq")
    half = message.shape[1] - (0 if reverse else 16)
    state = message.shape[2]
    if blocks != 8:
        local = message[:, :half].reshape(2 * half, state)
        if fades is None:
            fades = jnp.concatenate([read_fade(message[side, half:], per) for side in range(2)], 0)
        running = jnp.zeros((2 * half, state), F32)
        for _ in range(blocks - 1):
            running = shifted(faded(running, fades) + wide(local), "seq", -1 if reverse else 1)
        return low(running), fades
    side = lax.axis_index("seq") % 2
    even = side == 0
    mine = pick(message, side)
    other = exchange(pick(message, 1 - side), "seq", 1)
    first = jnp.where(even, mine, other)
    second = jnp.where(even, other, mine)
    if fades is None:
        fades = (read_fade(first[half:], per), read_fade(second[half:], per))
    first, second = wide(first[:half]), wide(second[:half])
    fade_first, fade_second = fades
    if reverse:
        total = faded(second, fade_first) + first
    else:
        total = faded(first, fade_second) + second
    sent = jnp.concatenate([low(total), fade_rows(fade_first * fade_second)], 0)
    sign = -1 if reverse else 1
    arrived = [shifted(sent, "seq", sign * 2 * hop) for hop in (1, 2, 3)]
    states = [wide(one[:half]) for one in arrived]
    factors = [read_fade(one[half:], per) for one in arrived]
    entering = states[0] + faded(states[1] + faded(states[2], factors[1]), factors[0])
    if reverse:
        for_second = entering
        for_first = second + faded(entering, fade_second)
    else:
        for_first = entering
        for_second = first + faded(entering, fade_first)
    for_first, for_second = low(for_first), low(for_second)
    kept = jnp.where(even, for_first, for_second)
    back = exchange(jnp.where(even, for_second, for_first), "seq", 1)
    return jnp.concatenate([jnp.where(even, kept, back), jnp.where(even, back, kept)], 0), fades


def layer_forward(entries, normed, rims, weights, next_gain):
    count = len(entries)
    inner = weights["w_z"].shape[1]
    channels = weights["conv"].shape[1]
    features = weights["w_out"].shape[1]
    state = (channels - inner) // 2
    length = entries[0].shape[0]
    heads = 2 * inner // LANES
    joined = [matmul(one, weights["w_in"]) for one in normed]
    if rims is None:
        before = [shifted(one[length - HALO :, :channels], "seq", 1) for one in joined]
    else:
        rim = matmul(rims, weights["w_in"])
        before = [rim[i * HALO : (i + 1) * HALO, :channels] for i in range(count)]
    gate = [matmul(one, weights["w_z"]) for one in normed]
    locals_ = [
        call(
            local_kernel,
            [
                ((length, inner), F32),
                ((2, inner // 2 + 16, state), BF16),
                ((length, state), BF16),
                ((length, LANES), F32),
            ],
            [((HALO + length, channels), F32), ((length, channels), F32)],
            3.2,
            joined[index], before[index], weights["conv"], weights["head"],
        )
        for index in range(count)
    ]
    scans = [scan_states(one[1], heads // 2, None, False) for one in locals_]
    finished = [
        call(
            output_kernel,
            [((length, inner), F32), ((length, features + LANES), BF16)],
            [((length, inner), BF16)],
            2.5,
            one[0], one[2], one[3], scan[0], gate[index], weights["mix"], weights["w_out"],
        )
        for index, (one, scan) in enumerate(zip(locals_, scans))
    ]
    outputs = []
    next_normed = []
    kept = []
    total_inner = inner * lax.axis_size("head")
    for index in range(count):
        ssd_out, part = finished[index]
        bit = 1
        while 2 * bit < lax.axis_size("head"):
            total = wide(part) + wide(exchange(part, "head", bit))
            squares = jnp.sum(total[:, features:], 1, keepdims=True)
            high = wide(low(squares))
            tail = jnp.pad(jnp.concatenate([high, squares - high], 1), ((0, 0), (0, LANES - 2)))
            part = low(jnp.concatenate([total[:, :features], tail], 1))
            bit *= 2
        out, branch, scale, later = call(
            functools.partial(merge_kernel, total_inner),
            [
                ((length, features), BF16),
                ((length, features), F32),
                ((length, LANES), F32),
                ((length, features), BF16),
            ],
            [],
            1.0,
            part, exchange(part, "head", bit), entries[index], next_gain,
        )
        outputs.append(out)
        next_normed.append(later)
        kept.append(
            dict(
                entry=entries[index], normed=normed[index],
                joined=joined[index], before=before[index], gate=gate[index],
                read=locals_[index][2], rise=locals_[index][3], start=scans[index][0],
                fades=scans[index][1], ssd_out=ssd_out, scale=scale, branch=branch,
            )
        )
    return outputs, next_normed, kept


def layer_backward(grads, lows, kept, weights):
    count = len(grads)
    inner = weights["w_z"].shape[1]
    channels = weights["conv"].shape[1]
    features = weights["w_out"].shape[1]
    state = (channels - inner) // 2
    length = grads[0].shape[0]
    heads = 2 * inner // LANES
    total_inner = inner * lax.axis_size("head")
    gates = []
    for grad_low, one in zip(lows, kept):
        gates.append(
            call(
                functools.partial(gate_back_kernel, total_inner),
                [
                    ((length, inner), F32),
                    ((length, inner), BF16),
                    ((length, inner), BF16),
                    ((2, inner // 2, state), BF16),
                    ((8, inner), F32),
                ],
                [],
                3.9,
                grad_low, weights["w_out"], one["ssd_out"], one["gate"], one["scale"],
                one["branch"], weights["mix"], one["rise"], one["read"],
            )
        )
    scans = [scan_states(gate[3], heads // 2, one["fades"], True)[0] for gate, one in zip(gates, kept)]
    mixes = [
        call(
            scan_back_kernel,
            [
                ((length, inner), F32),
                ((length, 2 * state), F32),
                ((length, 2 * LANES), F32),
                ((8, inner), F32),
            ],
            [
                ((HALO + length, channels), F32),
                ((length, channels), F32),
                ((LANES, length), F32),
                ((length, length), F32),
                ((length, inner), F32),
            ],
            1.0,
            one["joined"], one["before"], weights["conv"], weights["head"], gate[0], one["start"],
        )
        for gate, one in zip(gates, kept)
    ]
    states = [
        call(
            state_back_kernel,
            [
                ((length, channels), F32),
                ((length, LANES), BF16),
                ((8, channels), F32),
                ((8, LANES), F32),
            ],
            [((HALO + length, channels), F32), ((length, inner), F32)],
            4.1,
            one["joined"], one["before"], weights["conv"], weights["head"],
            mix[0], mix[1], mix[2], scan, one["start"],
        )
        for mix, scan, one in zip(mixes, scans, kept)
    ]
    after = [shifted(one[0][:HALO], "seq", -1) for one in states]
    inputs = [
        call(
            input_back_kernel,
            [((length, channels + LANES), BF16), ((length, features), BF16)],
            [((length + HALO, channels), F32)],
            2.0,
            one[0], rim, weights["conv"], one[1], gate[1], weights["w_in"], weights["w_z"],
        )
        for one, rim, gate in zip(states, after, gates)
    ]
    results = []
    for index in range(count):
        one = kept[index]
        part = inputs[index][1]
        bit = 1
        while 2 * bit < lax.axis_size("head"):
            part = low(wide(part) + wide(exchange(part, "head", bit)))
            bit *= 2
        results.append(
            call(
                entry_back_kernel,
                [((length, features), F32), ((length, features), BF16), ((8, features), F32)],
                [],
                1.2,
                part, exchange(part, "head", bit), one["entry"], weights["gain"], grads[index],
            )
        )
    pairs = (
        [one["normed"] for one in kept], lows, [one[0] for one in inputs], [one[1] for one in gates],
        [one[2] for one in gates], [one[2] for one in states], [one[3] for one in states],
        [one[4] for one in gates], [one[3] for one in mixes],
    )
    return results, reduced(pairs, [one[2] for one in results], inner, channels)


NAMES = (
    "norm_gain", "w_z", "w_x", "w_bc", "w_dt", "dt_bias", "a_log", "d_skip",
    "conv_x", "conv_bias_x", "conv_bc", "conv_bias_bc", "mix_gain", "w_out",
)


def packed(mine):
    inner = mine["w_z"].shape[1]
    lanes = lambda rows, width: jnp.pad(rows, ((0, 0), (0, width - rows.shape[1])))
    heads = mine["w_dt"].shape[1]
    w_in = jnp.concatenate([mine["w_x"], mine["w_bc"], lanes(mine["w_dt"], LANES)], 1)
    keys = mine["w_bc"].shape[1]
    bias = jnp.concatenate([mine["conv_bias_x"], mine["conv_bias_bc"]], 0)[None]
    skip = lanes(jnp.repeat(mine["d_skip"], inner // heads)[None], inner + keys)
    conv = jnp.concatenate([mine["conv_x"], mine["conv_bc"]], 1)
    rows = jnp.concatenate([conv, bias, skip, jnp.zeros((2, inner + keys), F32)], 0)
    head = lanes(jnp.stack([mine["dt_bias"], mine["a_log"]]), LANES)
    vectors = jnp.concatenate([lanes(head, LANES), jnp.zeros((6, LANES), F32)], 0)
    mix = jnp.pad(mine["mix_gain"][None], ((0, 7), (0, 0)))
    gain = jnp.pad(mine["norm_gain"][None], ((0, 7), (0, 0)))
    return dict(w_in=w_in, w_z=mine["w_z"], w_out=mine["w_out"], small=jnp.concatenate([rows, vectors, mix, gain], 1))


def both_layers(mine, hidden_in):
    first = lax.axis_index("section") == 0
    inner = mine["w_z"].shape[1]
    channels = inner + mine["w_bc"].shape[1]
    own = packed(mine)
    own["w_in"], hidden_in = lax.optimization_barrier((own["w_in"], hidden_in))
    other = {name: exchange(own[name], "section", 1) for name in ("small", "w_in")}
    own["w_z"], own["w_out"], other["w_in"] = lax.optimization_barrier(
        (own["w_z"], own["w_out"], other["w_in"])
    )
    other.update({name: exchange(own[name], "section", 1) for name in ("w_z", "w_out")})

    def layer(flag):
        chosen = {name: jnp.where(flag, own[name], other[name]) for name in own}
        small = chosen.pop("small")
        chosen["conv"] = small[:, :channels]
        chosen["head"] = small[:, channels : channels + LANES]
        chosen["mix"] = small[:, channels + LANES : channels + LANES + inner]
        chosen["gain"] = small[:, channels + LANES + inner :]
        return chosen

    return layer(first), layer(~first), hidden_in


def reduced(pairs, gains, inner, channels):
    section = lax.axis_index("section")
    length, features = pairs[0][0].shape
    half = features // 2
    width = channels + LANES + 2 * inner
    whole = lambda array: pl.BlockSpec(array.shape, lambda i, side: (0, 0))
    split = pl.BlockSpec((length, half), lambda i, side: (0, side[0]))
    flat = [array for pair in pairs for array in pair]

    def products(which):
        return pl.pallas_call(
            product_kernel,
            grid_spec=pltpu.PrefetchScalarGridSpec(
                num_scalar_prefetch=1,
                grid=(1,),
                in_specs=[split] * 4 + [whole(array) for array in flat[4:]],
                out_specs=pl.BlockSpec((half + 16, width), lambda i, side: (0, 0)),
            ),
            out_shape=jax.ShapeDtypeStruct((half + 16, width), BF16),
            compiler_params=pltpu.CompilerParams(vmem_limit_bytes=2 * VMEM),
            cost_estimate=pl.CostEstimate(flops=4 * 10**9, bytes_accessed=1 << 23, transcendentals=0),
        )(jnp.full((1,), which, jnp.int32), *flat)

    sent = products(1 - section)
    gain_sum = gains[0] + gains[1]
    gain_sum = gain_sum + exchange(gain_sum, "section", 1)
    rows = jnp.pad(gain_sum[0].reshape(-1, inner), ((0, 16 - features // inner), (0, 0)))
    other = exchange(sent, "section", 1)
    own = products(section)
    heads = lax.axis_size("head")
    if heads == 2:
        keys = exchange(own[:, inner:channels], "head", 1)
        route = [(i, i ^ 3) for i in range(4)]
        across = lax.ppermute(sent[:, inner:channels], ("section", "head"), route)
    else:
        mine = wide(own[:, inner:channels]) + wide(other[:, inner:channels])
        keys = low(head_sum(mine) - mine)
        across = jnp.zeros_like(keys)
    return call(
        functools.partial(add_kernel, inner, channels), [((half + 16, width - inner), BF16), ((half + 16, inner), BF16)],
        [], 3.0, own, other, keys, across, rows,
    )


def shards(hidden_in, order, cotangent, *params):
    mine = {name: param[0] for name, param in zip(NAMES, params)}
    *layers, hidden_in = both_layers(mine, hidden_in)
    sections = lax.axis_size("section")
    section = lax.axis_index("section")
    first = section == 0
    count = order.shape[0] // sections
    base = section * count
    inner = mine["w_z"].shape[1]
    channels = inner + mine["w_bc"].shape[1]
    features = hidden_in.shape[2]
    entries = [pick(hidden_in, order[base + index]) for index in range(count)]
    gains = [weights["gain"] for weights in layers]
    normed = [normalized(wide(entry), gains[0][0:1]) for entry in entries]
    rims = jnp.concatenate([entry[entry.shape[0] - HALO :] for entry in entries], 0)
    rims = normalized(wide(shifted(rims, "seq", 1)), gains[0][0:1])
    outputs = []
    kept = []
    for index, weights in enumerate(layers):
        entries, normed, one = layer_forward(entries, normed, rims if index == 0 else None, weights, gains[1])
        outputs.append(jnp.stack(entries))
        kept.append(one)
    incoming = [pick(cotangent, base + index) for index in range(count)]
    results, late = layer_backward(incoming, incoming, kept[1], layers[1])
    late_grads = jnp.stack([one[0] for one in results])
    wides = [one[0] for one in results]
    lows = [one[1] for one in results]
    late = lax.psum(late, "seq")

    def first_layer():
        results, early = layer_backward(lows, lows, kept[0], layers[0])
        return jnp.stack([one[0] for one in results]), *early

    def empty():
        return jnp.zeros(late_grads.shape, F32), *(jnp.zeros(one.shape, BF16) for one in late)

    early_grads, early, early_rest = lax.cond(order[0] >= 0, first_layer, empty)
    early, late = lax.optimization_barrier((early, late))
    early = lax.psum(early, "seq")
    late, late_rest = late
    if lax.axis_size("seq") * LANES <= inner:
        early_rest = lax.cond(
            order[0] >= 0, tree_sum, lambda part: jnp.zeros(part.shape, BF16), early_rest
        )
    else:
        early_rest = lax.psum(early_rest, "seq")

    def swapped(early, late):
        return exchange(jnp.where(first, late, early), "section", 1)

    def to_owner(early, late):
        own, sent = jnp.where(first, early, late), swapped(early, late)
        return jnp.concatenate([jnp.where(first, own, sent), jnp.where(first, sent, own)], 0)

    activations = to_owner(outputs[0], outputs[1])[None]
    grads = to_owner(early_grads, late_grads)[None]
    half = features // 2
    keys_width = channels - inner
    late_other = lax.ppermute(late, "section", [(0, 1)])
    late_rest_other = lax.ppermute(late_rest, "section", [(0, 1)])
    early_rest_other = lax.ppermute(early_rest, "section", [(1, 0)])
    early, late_other, late_rest_other, early_rest_other, activations, grads = lax.optimization_barrier(
        (early, late_other, late_rest_other, early_rest_other, activations, grads)
    )
    early_other = lax.ppermute(early, "section", [(1, 0)])
    keys_width = channels - inner
    early, late, activations, grads = lax.optimization_barrier((early, late, activations, grads))
    other = swapped(early, late)
    block = 128
    steps = half // block
    width = early.shape[1]
    place = lambda side, flag, i: (side[0] ^ flag) * steps + i
    shape = lambda rows, lanes: jax.ShapeDtypeStruct((rows, lanes), F32)

    def unpack(flag, parts, filled):
        given = lambda lanes: pl.BlockSpec((block, lanes), lambda i, side: (place(side, flag, i), 0))
        return pl.pallas_call(
            functools.partial(unpack_kernel, inner, keys_width),
            grid_spec=pltpu.PrefetchScalarGridSpec(
                num_scalar_prefetch=1,
                grid=(steps,),
                in_specs=[
                    pl.BlockSpec((block, width), lambda i, side: ((1 - side[0]) * i, 0)),
                    pl.BlockSpec((block, inner), lambda i, side: ((1 - side[0]) * i, 0)),
                    pl.BlockSpec((block, width), lambda i, side: (side[0] * i, 0)),
                    pl.BlockSpec((block, inner), lambda i, side: (side[0] * i, 0)),
                ]
                + [pl.BlockSpec(memory_space=pl.ANY)] * len(filled),
                out_specs=[
                    given(inner), given(keys_width), given(LANES), given(inner),
                    pl.BlockSpec((inner, block), lambda i, side: (0, place(side, flag, i))),
                ],
            ),
            out_shape=[
                shape(features, inner), shape(features, keys_width), shape(features, LANES),
                shape(features, inner), shape(inner, features),
            ],
            input_output_aliases={5 + i: i for i in range(len(filled))},
            compiler_params=pltpu.CompilerParams(vmem_limit_bytes=VMEM),
            cost_estimate=pl.CostEstimate(flops=5 * 10**9, bytes_accessed=1 << 23, transcendentals=0),
        )(jnp.full((1,), section, jnp.int32), *parts, *filled)

    filled = unpack(0, (early, early_rest, late, late_rest), [])
    others = (early_other, early_rest_other, late_other, late_rest_other)
    w_x, w_bc, w_dt, w_z, w_out = unpack(1, others, filled)
    rows = wide(jnp.where(first, early[half : half + 8], late[half : half + 8]))
    rest = wide(jnp.where(first, early_rest[half : half + 8], late_rest[half : half + 8]))
    heads = mine["w_dt"].shape[1]
    wide_in = channels + LANES
    mixes = rows[:, wide_in : wide_in + inner]
    gains = rest[: features // inner].reshape(features)
    results = dict(
        norm_gain=gains,
        w_z=w_z,
        w_x=w_x,
        w_bc=w_bc,
        w_dt=w_dt[:, :heads],
        dt_bias=rows[0, channels : channels + heads],
        a_log=rows[1, channels : channels + heads],
        d_skip=jnp.sum(mixes[1].reshape(heads, -1), 1),
        conv_x=rows[:4, :inner],
        conv_bias_x=rows[4, :inner],
        conv_bc=rows[:4, inner:channels],
        conv_bias_bc=rows[4, inner:channels],
        mix_gain=mixes[0],
        w_out=w_out,
    )
    return (activations, grads) + tuple(results[name][None] for name in NAMES)


def solution(mesh):
    in_specs = (
        P(None, "seq", None),
        P(),
        P(None, "seq", None),
        P("section", None),
        P("section", None, "head"),
        P("section", None, "head"),
        P("section", None, None),
        P("section", None, "head"),
        P("section", "head"),
        P("section", "head"),
        P("section", "head"),
        P("section", None, "head"),
        P("section", "head"),
        P("section", None, None),
        P("section", None),
        P("section", "head"),
        P("section", "head", None),
    )
    out_specs = (
        P("section", None, "seq", None),
        P("section", None, "seq", None),
        P("section", None),
        P("section", None, "head"),
        P("section", None, "head"),
        P("section", None, None),
        P("section", None, "head"),
        P("section", "head"),
        P("section", "head"),
        P("section", "head"),
        P("section", None, "head"),
        P("section", "head"),
        P("section", None, None),
        P("section", None),
        P("section", "head"),
        P("section", "head", None),
    )
    return jax.shard_map(shards, mesh=mesh, in_specs=in_specs, out_specs=out_specs, check_vma=False)
```

```python
import functools

import jax
import jax.numpy as jnp
from jax import lax
from jax.experimental import pallas as pl
from jax.experimental.pallas import tpu as pltpu
from jax.sharding import PartitionSpec as P

EPS = 1e-05
F32 = jnp.float32
BF16 = jnp.bfloat16
LANES = 128
HALO = 8
VMEM = 24 * 1024 * 1024


def exchange(block, axis, bit):
    route = [(i, i ^ bit) for i in range(lax.axis_size(axis))]
    return lax.ppermute(block, axis, route)


def shifted(block, axis, distance):
    devices = range(lax.axis_size(axis))
    route = [(i - distance, i) for i in devices if i - distance in devices]
    return lax.ppermute(block, axis, route)


def low(value):
    return value.astype(BF16)


def wide(value):
    return value.astype(F32)


def matmul(left, right):
    return jnp.dot(left, right, preferred_element_type=F32)


def lead_dot(left, right):
    return lax.dot_general(left, right, (((0,), (0,)), ((), ())), preferred_element_type=F32)


def tail_dot(left, right):
    return lax.dot_general(left, right, (((1,), (1,)), ((), ())), preferred_element_type=F32)


def head_sum(part):
    bit = 1
    while bit < lax.axis_size("head"):
        part = low(part)
        part = wide(part) + wide(exchange(part, "head", bit))
        bit *= 2
    return part


def parts_of(value, count):
    terms = []
    for _ in range(count):
        term = low(value)
        terms.append(term)
        value = value - wide(term)
    return terms


def dot_parts(left, right, count, dot=matmul):
    return sum(dot(left, term) for term in parts_of(right, count))


def iota(shape, axis):
    return lax.broadcasted_iota(jnp.int32, shape, axis)


def lower_mask(length):
    return iota((length, length), 0) >= iota((length, length), 1)


def expand(values, pair):
    length = values.shape[0]
    early = iota((length, LANES), 1) < LANES // 2
    first = values[:, 2 * pair : 2 * pair + 1]
    second = values[:, 2 * pair + 1 : 2 * pair + 2]
    return jnp.where(early, first, second)


def head_matrix(inner, width):
    return jnp.where(iota((inner, LANES), 0) // width == iota((inner, LANES), 1), 1.0, 0.0).astype(BF16)


def head_sums(values, matrix):
    high, rest = parts_of(values, 2)
    return matmul(high, matrix) + matmul(rest, matrix)


def sigmoid(value):
    return 1.0 / (1.0 + jnp.exp(-value))


def softplus(value):
    tail = jnp.exp(-jnp.abs(value))
    shifted_one = 1.0 + tail
    gap = shifted_one - 1.0
    small = jnp.where(gap == 0.0, tail, jnp.log(shifted_one) * (tail / jnp.where(gap == 0.0, 1.0, gap)))
    return jnp.maximum(value, 0.0) + small


def conv_preact(joined_ref, before_ref, conv_ref, ext_ref):
    length, channels = joined_ref.shape[0], conv_ref.shape[1]
    ext_ref[0:HALO, :] = before_ref[...]
    ext_ref[HALO : HALO + length, :] = joined_ref[:, 0:channels]
    total = conv_ref[4:5, :]
    for tap in range(4):
        total = total + conv_ref[tap : tap + 1, :] * ext_ref[HALO - 3 + tap : HALO - 3 + tap + length, :]
    return total


def decays(joined_ref, head_ref, channels):
    length = joined_ref.shape[0]
    raw = joined_ref[:, channels : channels + LANES] + head_ref[0:1, :]
    step = softplus(raw)
    rate = -jnp.exp(head_ref[1:2, :])
    lower = jnp.where(lower_mask(length), 1.0, 0.0).astype(BF16)
    decay_sum = dot_parts(lower, rate * step, 3)
    return raw, step, rate, decay_sum


def pair_dots(early, mixing_a, mixing_b, values, dot):
    return jnp.where(early, dot(mixing_a, values), dot(mixing_b, values))


def local_kernel(joined_ref, before_ref, conv_ref, head_ref, y_ref, message_ref, read_ref, rise_ref, ext_ref, act_ref):
    length = joined_ref.shape[0]
    channels = conv_ref.shape[1]
    inner = y_ref.shape[1]
    state = read_ref.shape[1]
    pairs = inner // LANES
    preact = conv_preact(joined_ref, before_ref, conv_ref, ext_ref)
    act_ref[...] = preact * sigmoid(preact)
    write_low = low(act_ref[:, inner : inner + state])
    read_low = low(act_ref[:, inner + state : inner + 2 * state])
    read_ref[...] = read_low
    _, step, _, decay_sum = decays(joined_ref, head_ref, channels)
    rise_ref[...] = jnp.exp(decay_sum)
    keep_step = jnp.exp(decay_sum[length - 1 : length, :] - decay_sum) * step
    decay_rows = decay_sum.T
    step_rows = step.T
    gram = tail_dot(read_low, write_low)
    lower = lower_mask(length)
    early = iota((length, LANES), 1) < LANES // 2
    half = inner // 2
    for pair in range(pairs):
        lanes = slice(pair * LANES, (pair + 1) * LANES)
        signal = act_ref[:, lanes]
        signal_low = low(signal)
        mixings = []
        for head in (2 * pair, 2 * pair + 1):
            diff = decay_sum[:, head : head + 1] - decay_rows[head : head + 1, :]
            decay = jnp.exp(jnp.where(lower, diff, -1e30))
            mixings.append(low(gram * decay * step_rows[head : head + 1, :]))
        mixed = pair_dots(early, mixings[0], mixings[1], signal_low, matmul)
        y_ref[:, lanes] = mixed + conv_ref[5:6, lanes] * signal
        local = lead_dot(low(expand(keep_step, pair) * signal), write_low)
        place = pair * LANES
        if half % LANES == 0:
            side, row = place // half, place % half
            message_ref[side, row : row + LANES, :] = low(local)
    heads = 2 * pairs
    per = heads // 2
    for side in range(2):
        column = jnp.exp(decay_rows[side * per : side * per + 8, length - 1 : length])
        fade = jnp.broadcast_to(column, (8, state))
        high = wide(low(fade))
        message_ref[side, half : half + 16, :] = low(jnp.concatenate([high, fade - high], 0))


def output_kernel(y_ref, read_ref, rise_ref, start_ref, gate_ref, mix_ref, w_ref, ssd_ref, part_ref, mixed_ref):
    length, inner = y_ref.shape
    features = w_ref.shape[1]
    squares = jnp.zeros((length, 1), F32)
    for pair in range(inner // LANES):
        lanes = slice(pair * LANES, (pair + 1) * LANES)
        reach = tail_dot(read_ref[...], start_ref[lanes, :])
        ssd_out = y_ref[:, lanes] + expand(rise_ref[...], pair) * reach
        ssd_ref[:, lanes] = ssd_out
        gate = gate_ref[:, lanes]
        gated = ssd_out * (gate * sigmoid(gate))
        squares = squares + jnp.sum(gated * gated, 1, keepdims=True)
        mixed_ref[:, lanes] = low(gated * mix_ref[0:1, lanes])
    part_ref[:, 0:features] = low(matmul(mixed_ref[...], w_ref[...]))
    high = wide(low(squares))
    lane = iota((length, LANES), 1)
    tail = jnp.where(lane == 0, high, jnp.where(lane == 1, squares - high, 0.0))
    part_ref[:, features : features + LANES] = low(tail)


def gate_back_kernel(
    total_inner, grad_ref, w_ref, ssd_ref, gate_ref, scale_ref, branch_ref, mix_ref, rise_ref, read_ref,
    grad_y_ref, gate_low_ref, mixed_ref, start_ref, sums_ref,
):
    length, inner = ssd_ref.shape
    scale = scale_ref[:, 0:1]
    along = jnp.sum(wide(grad_ref[...]) * branch_ref[...], 1, keepdims=True) * (scale * scale / total_inner)
    half = inner // 2
    sums_ref[...] = jnp.zeros(sums_ref.shape, F32)
    for pair in range(inner // LANES):
        lanes = slice(pair * LANES, (pair + 1) * LANES)
        grad_mixed = tail_dot(grad_ref[...], w_ref[lanes, :])
        gain = mix_ref[0:1, lanes]
        gate = gate_ref[:, lanes]
        ssd_out = ssd_ref[:, lanes]
        sigma = sigmoid(gate)
        active = gate * sigma
        gated = ssd_out * active
        normal = gated * scale
        sums_ref[0:1, lanes] = jnp.sum(grad_mixed * normal, 0, keepdims=True)
        mixed_ref[:, lanes] = low(normal * gain)
        grad_gated = scale * (grad_mixed * gain) - gated * along
        grad_y = grad_gated * active
        grad_y_ref[:, lanes] = grad_y
        gate_low_ref[:, lanes] = low(grad_gated * ssd_out * (sigma * (1.0 + gate * (1.0 - sigma))))
        grad_reach = low(grad_y * expand(rise_ref[...], pair))
        grad_start = lead_dot(grad_reach, read_ref[...])
        place = pair * LANES
        if half % LANES == 0:
            side, row = place // half, place % half
            start_ref[side, row : row + LANES, :] = low(grad_start)


def scan_back_kernel(
    joined_ref, before_ref, conv_ref, head_ref, grad_y_ref, start_ref,
    signal_ref, keys_ref, sums_ref, row_ref,
    ext_ref, act_ref, step_ref, gram_ref, prod_ref,
):
    length, inner = grad_y_ref.shape
    channels = conv_ref.shape[1]
    state = start_ref.shape[1]
    pairs = inner // LANES
    preact = conv_preact(joined_ref, before_ref, conv_ref, ext_ref)
    act_ref[...] = preact * sigmoid(preact)
    write_low = low(act_ref[:, inner : inner + state])
    read_low = low(act_ref[:, inner + state : inner + 2 * state])
    _, step, _, decay_sum = decays(joined_ref, head_ref, channels)
    rise = jnp.exp(decay_sum)
    decay_rows = decay_sum.T
    step_rows = step.T
    gram = tail_dot(read_low, write_low)
    lower = lower_mask(length)
    early = iota((length, LANES), 1) < LANES // 2
    lane = iota((length, LANES), 1)
    step_ref[...] = jnp.zeros(step_ref.shape, F32)
    gram_ref[...] = jnp.zeros(gram_ref.shape, F32)
    columns = jnp.zeros((length, LANES), F32)
    grad_read = jnp.zeros((length, state), F32)
    row_ref[...] = jnp.zeros(row_ref.shape, F32)
    for pair in range(pairs):
        lanes = slice(pair * LANES, (pair + 1) * LANES)
        signal = act_ref[:, lanes]
        signal_low = low(signal)
        grad_y = grad_y_ref[:, lanes]
        grad_y_low = low(grad_y)
        mixings = []
        for head in (2 * pair, 2 * pair + 1):
            mine = early if head % 2 == 0 else jnp.logical_not(early)
            own = jnp.where(mine, grad_y, 0.0)
            grad_mixing = tail_dot(low(own), signal_low)
            diff = decay_sum[:, head : head + 1] - decay_rows[head : head + 1, :]
            decay = jnp.exp(jnp.where(lower, diff, -1e30))
            step_row = step_rows[head : head + 1, :]
            plain = gram * decay
            mixings.append(low(plain * step_row))
            gram_ref[...] += grad_mixing * decay * step_row
            weighed = grad_mixing * plain
            step_ref[head : head + 1, :] = jnp.sum(weighed, 0, keepdims=True)
            columns = jnp.where(lane == head, jnp.sum(weighed * step_row, 1, keepdims=True), columns)
        back = pair_dots(early, mixings[0], mixings[1], grad_y_low, lead_dot)
        signal_ref[:, lanes] = conv_ref[5:6, lanes] * grad_y + back
        row_ref[0:1, lanes] = jnp.sum(grad_y * signal, 0, keepdims=True)
        start = start_ref[lanes, :]
        reach = tail_dot(read_low, start)
        prod_ref[:, lanes] = grad_y * reach
        grad_read = grad_read + matmul(low(grad_y * expand(rise, pair)), start)
    gram_parts = parts_of(gram_ref[...], 2)
    keys_ref[:, 0:state] = sum(lead_dot(part, read_low) for part in gram_parts)
    keys_ref[:, state : 2 * state] = grad_read + sum(matmul(part, write_low) for part in gram_parts)
    grad_step = step_ref[...].T
    matrix = head_matrix(inner, LANES // 2)
    sums_ref[:, 0:LANES] = columns - step * grad_step + head_sums(prod_ref[...], matrix) * rise
    sums_ref[:, LANES : 2 * LANES] = grad_step


def state_back_kernel(
    joined_ref, before_ref, conv_ref, head_ref, signal_ref, keys_ref, sums_ref, local_ref, start_ref,
    pre_ref, raw_ref, conv_sums_ref, head_sums_ref,
    ext_ref, prod_ref,
):
    length, inner = signal_ref.shape
    channels = conv_ref.shape[1]
    state = start_ref.shape[1]
    preact = conv_preact(joined_ref, before_ref, conv_ref, ext_ref)
    raw, step, rate, decay_sum = decays(joined_ref, head_ref, channels)
    keep = jnp.exp(decay_sum[length - 1 : length, :] - decay_sum)
    tail = keep * step
    sigma = sigmoid(preact)
    active = preact * sigma
    slope = sigma * (1.0 + preact * (1.0 - sigma))
    write_low = low(active[:, inner : inner + state])
    grad_write = keys_ref[:, 0:state]
    conv_sums_ref[...] = jnp.zeros(conv_sums_ref.shape, F32)

    def finish(grad, lanes):
        grad_pre = grad * slope[:, lanes]
        pre_ref[:, lanes] = grad_pre
        for tap in range(4):
            rows = ext_ref[HALO - 3 + tap : HALO - 3 + tap + length, lanes]
            conv_sums_ref[tap : tap + 1, lanes] = jnp.sum(grad_pre * rows, 0, keepdims=True)
        conv_sums_ref[4:5, lanes] = jnp.sum(grad_pre, 0, keepdims=True)

    for pair in range(inner // LANES):
        lanes = slice(pair * LANES, (pair + 1) * LANES)
        signal = active[:, lanes]
        local = local_ref[lanes, :]
        spread = tail_dot(write_low, local)
        wide_tail = expand(tail, pair)
        prod_ref[:, lanes] = signal * spread
        grad_write = grad_write + matmul(low(wide_tail * signal), local)
        finish(signal_ref[:, lanes] + wide_tail * spread, lanes)
    finish(grad_write, slice(inner, inner + state))
    finish(keys_ref[:, state : 2 * state], slice(inner + state, inner + 2 * state))
    matrix = head_matrix(inner, LANES // 2)
    grad_tail = head_sums(prod_ref[...], matrix)
    grad_step = sums_ref[:, LANES : 2 * LANES] + grad_tail * keep
    tail_log = grad_tail * tail
    product = wide(local_ref[...]) * wide(start_ref[...])
    by_state = sum(lead_dot(matrix, part) for part in parts_of(product, 2))
    ones = jnp.ones((8, state), BF16)
    totals = sum(tail_dot(ones, part) for part in parts_of(by_state, 2))[0:1, :]
    fade = jnp.exp(decay_sum[length - 1 : length, :])
    last = iota((length, LANES), 0) == length - 1
    extra = jnp.sum(tail_log, 0, keepdims=True) + totals * fade
    grad_decay = sums_ref[:, 0:LANES] - tail_log + jnp.where(last, extra, 0.0)
    upper = jnp.where(iota((length, length), 1) >= iota((length, length), 0), 1.0, 0.0).astype(BF16)
    grad_log = dot_parts(upper, grad_decay, 3)
    grad_step = grad_step + grad_log * rate
    grad_raw = grad_step * sigmoid(raw)
    raw_ref[...] = low(grad_raw)
    head_sums_ref[...] = jnp.zeros(head_sums_ref.shape, F32)
    head_sums_ref[0:1, :] = jnp.sum(grad_raw, 0, keepdims=True)
    head_sums_ref[1:2, :] = jnp.sum(grad_log * step, 0, keepdims=True) * rate


def input_back_kernel(pre_ref, after_ref, conv_ref, raw_ref, gate_ref, w_ref, w_gate_ref, joined_ref, part_ref, ext_ref):
    length, channels = pre_ref.shape
    ext_ref[0:length, :] = pre_ref[...]
    ext_ref[length : length + HALO, :] = after_ref[...]
    total = jnp.zeros((length, channels), F32)
    for tap in range(4):
        total = total + conv_ref[tap : tap + 1, :] * ext_ref[3 - tap : 3 - tap + length, :]
    joined_ref[:, 0:channels] = low(total)
    joined_ref[:, channels : channels + LANES] = raw_ref[...]
    part_ref[...] = low(tail_dot(joined_ref[...], w_ref[...]) + tail_dot(gate_ref[...], w_gate_ref[...]))


def normalized(value, gain):
    return low(value * lax.rsqrt(jnp.mean(value * value, 1, keepdims=True) + EPS) * gain)


def merge_kernel(total_inner, part_ref, other_ref, entry_ref, gain_ref, out_ref, branch_ref, scale_ref, normed_ref):
    features = entry_ref.shape[1]
    total = wide(part_ref[...]) + wide(other_ref[...])
    squares = jnp.sum(total[:, features:], 1, keepdims=True)
    scale = lax.rsqrt(squares / total_inner + EPS)
    branch = scale * total[:, :features]
    out = low(wide(entry_ref[...]) + branch)
    out_ref[...] = out
    branch_ref[...] = branch
    scale_ref[...] = jnp.broadcast_to(scale, scale_ref.shape)
    normed_ref[...] = normalized(wide(out), gain_ref[0:1, :])


def entry_back_kernel(part_ref, other_ref, entry_ref, gain_ref, grad_ref, out_ref, low_ref, sums_ref):
    grad_normed = wide(part_ref[...]) + wide(other_ref[...])
    value = wide(entry_ref[...])
    inverse_rms = lax.rsqrt(jnp.mean(value * value, 1, keepdims=True) + EPS)
    sums_ref[...] = jnp.zeros(sums_ref.shape, F32)
    sums_ref[0:1, :] = jnp.sum(grad_normed * value * inverse_rms, 0, keepdims=True)
    scaled = grad_normed * gain_ref[0:1, :]
    mean = jnp.mean(scaled * value, 1, keepdims=True)
    out = wide(grad_ref[...]) + inverse_rms * scaled - value * (inverse_rms * inverse_rms * inverse_rms * mean)
    out_ref[...] = out
    low_ref[...] = low(out)


def product_kernel(
    half_ref, normed_a, normed_b, grad_a, grad_b, joined_a, joined_b, gate_a, gate_b, mixed_a, mixed_b,
    conv_a, conv_b, head_a, head_b, mix_a, mix_b, skip_a, skip_b, out_ref,
):
    rows = normed_a.shape[1]
    wide_in, inner = joined_a.shape[1], gate_a.shape[1]
    channels = wide_in - LANES
    gate_at, out_at = wide_in, wide_in + inner
    both = lambda left_a, right_a, left_b, right_b: low(
        lead_dot(left_a[...], right_a[...]) + lead_dot(left_b[...], right_b[...])
    )
    out_ref[0:rows, 0:wide_in] = both(normed_a, joined_a, normed_b, joined_b)
    out_ref[0:rows, gate_at:out_at] = both(normed_a, gate_a, normed_b, gate_b)
    out_ref[0:rows, out_at : out_at + inner] = both(grad_a, mixed_a, grad_b, mixed_b)
    pad = lambda value: low(jnp.concatenate([value, jnp.zeros(value.shape, F32)], 0))
    last = slice(rows, rows + 16)
    out_ref[last, 0:channels] = pad(conv_a[...] + conv_b[...])
    out_ref[last, channels:wide_in] = pad(head_a[...] + head_b[...])
    place = iota((8, inner), 0)
    mixes = mix_a[0:1, :] + mix_b[0:1, :]
    skips = skip_a[0:1, :] + skip_b[0:1, :]
    out_ref[last, gate_at:out_at] = pad(jnp.where(place == 0, mixes, jnp.where(place == 1, skips, 0.0)))
    out_ref[last, out_at : out_at + inner] = jnp.zeros((16, inner), BF16)


def add_kernel(inner, channels, own_ref, other_ref, keys_ref, gains_ref, out_ref, rest_ref):
    step = 48
    half, cut = own_ref.shape[0] - 16, out_ref.shape[1]
    for at in range(0, own_ref.shape[0], step):
        rows = slice(at, at + step)
        total = wide(own_ref[rows, :]) + wide(other_ref[rows, :])
        out_ref[rows, :] = low(total[:, :cut])
        rest_ref[rows, :] = low(total[:, cut:])
        out_ref[rows, inner:channels] = keys_ref[rows, :]
    rest_ref[half : half + 16, :] = low(gains_ref[...])


def unpack_kernel(inner, keys, section_ref, early_ref, early_rest_ref, late_ref, late_rest_ref, *refs):
    x_ref, keys_ref, step_ref, gate_ref, out_ref = refs[-5:]
    value = wide(jnp.where(section_ref[0] == 0, early_ref[...], late_ref[...]))
    wide_in = inner + keys + LANES
    x_ref[...] = value[:, :inner]
    keys_ref[...] = value[:, inner : inner + keys]
    step_ref[...] = value[:, inner + keys : wide_in]
    gate_ref[...] = value[:, wide_in : wide_in + inner]
    rest = jnp.where(section_ref[0] == 0, early_rest_ref[...], late_rest_ref[...])
    out_ref[...] = wide(rest).T


def call(kernel, outs, scratch, micros, *args):
    shapes = [jax.ShapeDtypeStruct(shape, dtype) for shape, dtype in outs]
    moved = sum(a.size * a.dtype.itemsize for a in args) + sum(s.size * s.dtype.itemsize for s in shapes)
    return pl.pallas_call(
        kernel,
        out_shape=shapes,
        in_specs=[pl.BlockSpec(memory_space=pltpu.VMEM)] * len(args),
        out_specs=[pl.BlockSpec(memory_space=pltpu.VMEM)] * len(shapes),
        scratch_shapes=[pltpu.VMEM(shape, dtype) for shape, dtype in scratch],
        compiler_params=pltpu.CompilerParams(vmem_limit_bytes=VMEM),
        cost_estimate=pl.CostEstimate(flops=int(micros * 1.1e9), bytes_accessed=moved, transcendentals=0),
    )(*args)


def pick(halves, index):
    return lax.dynamic_index_in_dim(halves, index, 0, False)


def faded(state, fade):
    per = fade.shape[0]
    rows, lanes = state.shape
    return (state.reshape(per, rows // per, lanes) * fade[:, None, :]).reshape(rows, lanes)


def fade_rows(fade):
    per = fade.shape[0]
    high = wide(low(fade))
    pad = lambda rows: jnp.pad(rows, ((0, 8 - per), (0, 0)))
    return low(jnp.concatenate([pad(high), pad(fade - high)], 0))


def read_fade(rows, per):
    return wide(rows[:per]) + wide(rows[8 : 8 + per])


def tree_sum(part):
    me = lax.axis_index("seq")
    bit = 1
    while bit < lax.axis_size("seq"):
        half = part.shape[1] // 2
        upper = (me & bit) != 0
        left, right = part[:, :half], part[:, half:]
        sent = jnp.where(upper, left, right)
        part = low(wide(jnp.where(upper, right, left)) + wide(exchange(sent, "seq", bit)))
        bit *= 2
    while bit > 1:
        bit //= 2
        upper = (me & bit) != 0
        other = exchange(part, "seq", bit)
        part = jnp.concatenate([jnp.where(upper, other, part), jnp.where(upper, part, other)], 1)
    return part


def scan_states(message, per, fades, reverse):
    blocks = lax.axis_size("seq")
    half = message.shape[1] - (0 if reverse else 16)
    state = message.shape[2]
    if blocks != 8:
        local = message[:, :half].reshape(2 * half, state)
        if fades is None:
            fades = jnp.concatenate([read_fade(message[side, half:], per) for side in range(2)], 0)
        running = jnp.zeros((2 * half, state), F32)
        for _ in range(blocks - 1):
            running = shifted(faded(running, fades) + wide(local), "seq", -1 if reverse else 1)
        return low(running), fades
    side = lax.axis_index("seq") % 2
    even = side == 0
    mine = pick(message, side)
    other = exchange(pick(message, 1 - side), "seq", 1)
    first = jnp.where(even, mine, other)
    second = jnp.where(even, other, mine)
    if fades is None:
        fades = (read_fade(first[half:], per), read_fade(second[half:], per))
    first, second = wide(first[:half]), wide(second[:half])
    fade_first, fade_second = fades
    if reverse:
        total = faded(second, fade_first) + first
    else:
        total = faded(first, fade_second) + second
    sent = jnp.concatenate([low(total), fade_rows(fade_first * fade_second)], 0)
    sign = -1 if reverse else 1
    arrived = [shifted(sent, "seq", sign * 2 * hop) for hop in (1, 2, 3)]
    states = [wide(one[:half]) for one in arrived]
    factors = [read_fade(one[half:], per) for one in arrived]
    entering = states[0] + faded(states[1] + faded(states[2], factors[1]), factors[0])
    if reverse:
        for_second = entering
        for_first = second + faded(entering, fade_second)
    else:
        for_first = entering
        for_second = first + faded(entering, fade_first)
    for_first, for_second = low(for_first), low(for_second)
    kept = jnp.where(even, for_first, for_second)
    back = exchange(jnp.where(even, for_second, for_first), "seq", 1)
    return jnp.concatenate([jnp.where(even, kept, back), jnp.where(even, back, kept)], 0), fades


def layer_forward(entries, normed, rims, weights, next_gain):
    count = len(entries)
    inner = weights["w_z"].shape[1]
    channels = weights["conv"].shape[1]
    features = weights["w_out"].shape[1]
    state = (channels - inner) // 2
    length = entries[0].shape[0]
    heads = 2 * inner // LANES
    joined = [matmul(one, weights["w_in"]) for one in normed]
    if rims is None:
        before = [shifted(one[length - HALO :, :channels], "seq", 1) for one in joined]
    else:
        rim = matmul(rims, weights["w_in"])
        before = [rim[i * HALO : (i + 1) * HALO, :channels] for i in range(count)]
    gate = [matmul(one, weights["w_z"]) for one in normed]
    locals_ = [
        call(
            local_kernel,
            [
                ((length, inner), F32),
                ((2, inner // 2 + 16, state), BF16),
                ((length, state), BF16),
                ((length, LANES), F32),
            ],
            [((HALO + length, channels), F32), ((length, channels), F32)],
            3.2,
            joined[index], before[index], weights["conv"], weights["head"],
        )
        for index in range(count)
    ]
    scans = [scan_states(one[1], heads // 2, None, False) for one in locals_]
    finished = [
        call(
            output_kernel,
            [((length, inner), F32), ((length, features + LANES), BF16)],
            [((length, inner), BF16)],
            2.5,
            one[0], one[2], one[3], scan[0], gate[index], weights["mix"], weights["w_out"],
        )
        for index, (one, scan) in enumerate(zip(locals_, scans))
    ]
    outputs = []
    next_normed = []
    kept = []
    total_inner = inner * lax.axis_size("head")
    for index in range(count):
        ssd_out, part = finished[index]
        bit = 1
        while 2 * bit < lax.axis_size("head"):
            total = wide(part) + wide(exchange(part, "head", bit))
            squares = jnp.sum(total[:, features:], 1, keepdims=True)
            high = wide(low(squares))
            tail = jnp.pad(jnp.concatenate([high, squares - high], 1), ((0, 0), (0, LANES - 2)))
            part = low(jnp.concatenate([total[:, :features], tail], 1))
            bit *= 2
        out, branch, scale, later = call(
            functools.partial(merge_kernel, total_inner),
            [
                ((length, features), BF16),
                ((length, features), F32),
                ((length, LANES), F32),
                ((length, features), BF16),
            ],
            [],
            1.0,
            part, exchange(part, "head", bit), entries[index], next_gain,
        )
        outputs.append(out)
        next_normed.append(later)
        kept.append(
            dict(
                entry=entries[index], normed=normed[index],
                joined=joined[index], before=before[index], gate=gate[index],
                read=locals_[index][2], rise=locals_[index][3], start=scans[index][0],
                fades=scans[index][1], ssd_out=ssd_out, scale=scale, branch=branch,
            )
        )
    return outputs, next_normed, kept


def layer_backward(grads, lows, kept, weights):
    count = len(grads)
    inner = weights["w_z"].shape[1]
    channels = weights["conv"].shape[1]
    features = weights["w_out"].shape[1]
    state = (channels - inner) // 2
    length = grads[0].shape[0]
    heads = 2 * inner // LANES
    total_inner = inner * lax.axis_size("head")
    gates = []
    for grad_low, one in zip(lows, kept):
        gates.append(
            call(
                functools.partial(gate_back_kernel, total_inner),
                [
                    ((length, inner), F32),
                    ((length, inner), BF16),
                    ((length, inner), BF16),
                    ((2, inner // 2, state), BF16),
                    ((8, inner), F32),
                ],
                [],
                3.9,
                grad_low, weights["w_out"], one["ssd_out"], one["gate"], one["scale"],
                one["branch"], weights["mix"], one["rise"], one["read"],
            )
        )
    scans = [scan_states(gate[3], heads // 2, one["fades"], True)[0] for gate, one in zip(gates, kept)]
    mixes = [
        call(
            scan_back_kernel,
            [
                ((length, inner), F32),
                ((length, 2 * state), F32),
                ((length, 2 * LANES), F32),
                ((8, inner), F32),
            ],
            [
                ((HALO + length, channels), F32),
                ((length, channels), F32),
                ((LANES, length), F32),
                ((length, length), F32),
                ((length, inner), F32),
            ],
            1.0,
            one["joined"], one["before"], weights["conv"], weights["head"], gate[0], one["start"],
        )
        for gate, one in zip(gates, kept)
    ]
    states = [
        call(
            state_back_kernel,
            [
                ((length, channels), F32),
                ((length, LANES), BF16),
                ((8, channels), F32),
                ((8, LANES), F32),
            ],
            [((HALO + length, channels), F32), ((length, inner), F32)],
            4.1,
            one["joined"], one["before"], weights["conv"], weights["head"],
            mix[0], mix[1], mix[2], scan, one["start"],
        )
        for mix, scan, one in zip(mixes, scans, kept)
    ]
    after = [shifted(one[0][:HALO], "seq", -1) for one in states]
    inputs = [
        call(
            input_back_kernel,
            [((length, channels + LANES), BF16), ((length, features), BF16)],
            [((length + HALO, channels), F32)],
            2.0,
            one[0], rim, weights["conv"], one[1], gate[1], weights["w_in"], weights["w_z"],
        )
        for one, rim, gate in zip(states, after, gates)
    ]
    results = []
    for index in range(count):
        one = kept[index]
        part = inputs[index][1]
        bit = 1
        while 2 * bit < lax.axis_size("head"):
            part = low(wide(part) + wide(exchange(part, "head", bit)))
            bit *= 2
        results.append(
            call(
                entry_back_kernel,
                [((length, features), F32), ((length, features), BF16), ((8, features), F32)],
                [],
                1.2,
                part, exchange(part, "head", bit), one["entry"], weights["gain"], grads[index],
            )
        )
    pairs = (
        [one["normed"] for one in kept], lows, [one[0] for one in inputs], [one[1] for one in gates],
        [one[2] for one in gates], [one[2] for one in states], [one[3] for one in states],
        [one[4] for one in gates], [one[3] for one in mixes],
    )
    return results, reduced(pairs, [one[2] for one in results], inner, channels)


NAMES = (
    "norm_gain", "w_z", "w_x", "w_bc", "w_dt", "dt_bias", "a_log", "d_skip",
    "conv_x", "conv_bias_x", "conv_bc", "conv_bias_bc", "mix_gain", "w_out",
)


def packed(mine):
    inner = mine["w_z"].shape[1]
    lanes = lambda rows, width: jnp.pad(rows, ((0, 0), (0, width - rows.shape[1])))
    heads = mine["w_dt"].shape[1]
    w_in = jnp.concatenate([mine["w_x"], mine["w_bc"], lanes(mine["w_dt"], LANES)], 1)
    keys = mine["w_bc"].shape[1]
    bias = jnp.concatenate([mine["conv_bias_x"], mine["conv_bias_bc"]], 0)[None]
    skip = lanes(jnp.repeat(mine["d_skip"], inner // heads)[None], inner + keys)
    conv = jnp.concatenate([mine["conv_x"], mine["conv_bc"]], 1)
    rows = jnp.concatenate([conv, bias, skip, jnp.zeros((2, inner + keys), F32)], 0)
    head = lanes(jnp.stack([mine["dt_bias"], mine["a_log"]]), LANES)
    vectors = jnp.concatenate([lanes(head, LANES), jnp.zeros((6, LANES), F32)], 0)
    mix = jnp.pad(mine["mix_gain"][None], ((0, 7), (0, 0)))
    gain = jnp.pad(mine["norm_gain"][None], ((0, 7), (0, 0)))
    return dict(w_in=w_in, w_z=mine["w_z"], w_out=mine["w_out"], small=jnp.concatenate([rows, vectors, mix, gain], 1))


def both_layers(mine, hidden_in):
    first = lax.axis_index("section") == 0
    inner = mine["w_z"].shape[1]
    channels = inner + mine["w_bc"].shape[1]
    own = packed(mine)
    own["w_in"], hidden_in = lax.optimization_barrier((own["w_in"], hidden_in))
    other = {name: exchange(own[name], "section", 1) for name in ("small", "w_in")}
    own["w_z"], own["w_out"], other["w_in"] = lax.optimization_barrier(
        (own["w_z"], own["w_out"], other["w_in"])
    )
    other.update({name: exchange(own[name], "section", 1) for name in ("w_z", "w_out")})

    def layer(flag):
        chosen = {name: jnp.where(flag, own[name], other[name]) for name in own}
        small = chosen.pop("small")
        chosen["conv"] = small[:, :channels]
        chosen["head"] = small[:, channels : channels + LANES]
        chosen["mix"] = small[:, channels + LANES : channels + LANES + inner]
        chosen["gain"] = small[:, channels + LANES + inner :]
        return chosen

    return layer(first), layer(~first), hidden_in


def reduced(pairs, gains, inner, channels):
    section = lax.axis_index("section")
    length, features = pairs[0][0].shape
    half = features // 2
    width = channels + LANES + 2 * inner
    whole = lambda array: pl.BlockSpec(array.shape, lambda i, side: (0, 0))
    split = pl.BlockSpec((length, half), lambda i, side: (0, side[0]))
    flat = [array for pair in pairs for array in pair]

    def products(which):
        return pl.pallas_call(
            product_kernel,
            grid_spec=pltpu.PrefetchScalarGridSpec(
                num_scalar_prefetch=1,
                grid=(1,),
                in_specs=[split] * 4 + [whole(array) for array in flat[4:]],
                out_specs=pl.BlockSpec((half + 16, width), lambda i, side: (0, 0)),
            ),
            out_shape=jax.ShapeDtypeStruct((half + 16, width), BF16),
            compiler_params=pltpu.CompilerParams(vmem_limit_bytes=2 * VMEM),
            cost_estimate=pl.CostEstimate(flops=4 * 10**9, bytes_accessed=1 << 23, transcendentals=0),
        )(jnp.full((1,), which, jnp.int32), *flat)

    sent = products(1 - section)
    gain_sum = gains[0] + gains[1]
    gain_sum = gain_sum + exchange(gain_sum, "section", 1)
    rows = jnp.pad(gain_sum[0].reshape(-1, inner), ((0, 16 - features // inner), (0, 0)))
    other = exchange(sent, "section", 1)
    own = products(section)
    keys = low(head_sum(wide(own[:, inner:channels]) + wide(other[:, inner:channels])))
    return call(
        functools.partial(add_kernel, inner, channels), [((half + 16, width - inner), BF16), ((half + 16, inner), BF16)],
        [], 3.0, own, other, keys, rows,
    )


def shards(hidden_in, order, cotangent, *params):
    mine = {name: param[0] for name, param in zip(NAMES, params)}
    *layers, hidden_in = both_layers(mine, hidden_in)
    sections = lax.axis_size("section")
    section = lax.axis_index("section")
    first = section == 0
    count = order.shape[0] // sections
    base = section * count
    inner = mine["w_z"].shape[1]
    channels = inner + mine["w_bc"].shape[1]
    features = hidden_in.shape[2]
    entries = [pick(hidden_in, order[base + index]) for index in range(count)]
    gains = [weights["gain"] for weights in layers]
    normed = [normalized(wide(entry), gains[0][0:1]) for entry in entries]
    rims = jnp.concatenate([entry[entry.shape[0] - HALO :] for entry in entries], 0)
    rims = normalized(wide(shifted(rims, "seq", 1)), gains[0][0:1])
    outputs = []
    kept = []
    for index, weights in enumerate(layers):
        entries, normed, one = layer_forward(entries, normed, rims if index == 0 else None, weights, gains[1])
        outputs.append(jnp.stack(entries))
        kept.append(one)
    incoming = [pick(cotangent, base + index) for index in range(count)]
    results, late = layer_backward(incoming, incoming, kept[1], layers[1])
    late_grads = jnp.stack([one[0] for one in results])
    wides = [one[0] for one in results]
    lows = [one[1] for one in results]
    late = lax.psum(late, "seq")

    def first_layer():
        results, early = layer_backward(lows, lows, kept[0], layers[0])
        return jnp.stack([one[0] for one in results]), *early

    def empty():
        return jnp.zeros(late_grads.shape, F32), *(jnp.zeros(one.shape, BF16) for one in late)

    early_grads, early, early_rest = lax.cond(order[0] >= 0, first_layer, empty)
    early, late = lax.optimization_barrier((early, late))
    early = lax.psum(early, "seq")
    late, late_rest = late
    if lax.axis_size("seq") * LANES <= inner:
        early_rest = lax.cond(
            order[0] >= 0, tree_sum, lambda part: jnp.zeros(part.shape, BF16), early_rest
        )
    else:
        early_rest = lax.psum(early_rest, "seq")

    def swapped(early, late):
        return exchange(jnp.where(first, late, early), "section", 1)

    def to_owner(early, late):
        own, sent = jnp.where(first, early, late), swapped(early, late)
        return jnp.concatenate([jnp.where(first, own, sent), jnp.where(first, sent, own)], 0)

    activations = to_owner(outputs[0], outputs[1])[None]
    grads = to_owner(early_grads, late_grads)[None]
    half = features // 2
    keys_width = channels - inner
    late_other = lax.ppermute(late, "section", [(0, 1)])
    late_rest_other = lax.ppermute(late_rest, "section", [(0, 1)])
    early_rest_other = lax.ppermute(early_rest, "section", [(1, 0)])
    early, late_other, late_rest_other, early_rest_other, activations, grads = lax.optimization_barrier(
        (early, late_other, late_rest_other, early_rest_other, activations, grads)
    )
    early_other = lax.ppermute(early, "section", [(1, 0)])
    keys_width = channels - inner
    early, late, activations, grads = lax.optimization_barrier((early, late, activations, grads))
    other = swapped(early, late)
    block = 128
    steps = half // block
    width = early.shape[1]
    place = lambda side, flag, i: (side[0] ^ flag) * steps + i
    shape = lambda rows, lanes: jax.ShapeDtypeStruct((rows, lanes), F32)

    def unpack(flag, parts, filled):
        given = lambda lanes: pl.BlockSpec((block, lanes), lambda i, side: (place(side, flag, i), 0))
        return pl.pallas_call(
            functools.partial(unpack_kernel, inner, keys_width),
            grid_spec=pltpu.PrefetchScalarGridSpec(
                num_scalar_prefetch=1,
                grid=(steps,),
                in_specs=[
                    pl.BlockSpec((block, width), lambda i, side: ((1 - side[0]) * i, 0)),
                    pl.BlockSpec((block, inner), lambda i, side: ((1 - side[0]) * i, 0)),
                    pl.BlockSpec((block, width), lambda i, side: (side[0] * i, 0)),
                    pl.BlockSpec((block, inner), lambda i, side: (side[0] * i, 0)),
                ]
                + [pl.BlockSpec(memory_space=pl.ANY)] * len(filled),
                out_specs=[
                    given(inner), given(keys_width), given(LANES), given(inner),
                    pl.BlockSpec((inner, block), lambda i, side: (0, place(side, flag, i))),
                ],
            ),
            out_shape=[
                shape(features, inner), shape(features, keys_width), shape(features, LANES),
                shape(features, inner), shape(inner, features),
            ],
            input_output_aliases={5 + i: i for i in range(len(filled))},
            compiler_params=pltpu.CompilerParams(vmem_limit_bytes=VMEM),
            cost_estimate=pl.CostEstimate(flops=5 * 10**9, bytes_accessed=1 << 23, transcendentals=0),
        )(jnp.full((1,), section, jnp.int32), *parts, *filled)

    filled = unpack(0, (early, early_rest, late, late_rest), [])
    others = (early_other, early_rest_other, late_other, late_rest_other)
    w_x, w_bc, w_dt, w_z, w_out = unpack(1, others, filled)
    rows = wide(jnp.where(first, early[half : half + 8], late[half : half + 8]))
    rest = wide(jnp.where(first, early_rest[half : half + 8], late_rest[half : half + 8]))
    heads = mine["w_dt"].shape[1]
    wide_in = channels + LANES
    mixes = rows[:, wide_in : wide_in + inner]
    gains = rest[: features // inner].reshape(features)
    results = dict(
        norm_gain=gains,
        w_z=w_z,
        w_x=w_x,
        w_bc=w_bc,
        w_dt=w_dt[:, :heads],
        dt_bias=rows[0, channels : channels + heads],
        a_log=rows[1, channels : channels + heads],
        d_skip=jnp.sum(mixes[1].reshape(heads, -1), 1),
        conv_x=rows[:4, :inner],
        conv_bias_x=rows[4, :inner],
        conv_bc=rows[:4, inner:channels],
        conv_bias_bc=rows[4, inner:channels],
        mix_gain=mixes[0],
        w_out=w_out,
    )
    return (activations, grads) + tuple(results[name][None] for name in NAMES)


def solution(mesh):
    in_specs = (
        P(None, "seq", None),
        P(),
        P(None, "seq", None),
        P("section", None),
        P("section", None, "head"),
        P("section", None, "head"),
        P("section", None, None),
        P("section", None, "head"),
        P("section", "head"),
        P("section", "head"),
        P("section", "head"),
        P("section", None, "head"),
        P("section", "head"),
        P("section", None, None),
        P("section", None),
        P("section", "head"),
        P("section", "head", None),
    )
    out_specs = (
        P("section", None, "seq", None),
        P("section", None, "seq", None),
        P("section", None),
        P("section", None, "head"),
        P("section", None, "head"),
        P("section", None, None),
        P("section", None, "head"),
        P("section", "head"),
        P("section", "head"),
        P("section", "head"),
        P("section", None, "head"),
        P("section", "head"),
        P("section", None, None),
        P("section", None),
        P("section", "head"),
        P("section", "head", None),
    )
    return jax.shard_map(shards, mesh=mesh, in_specs=in_specs, out_specs=out_specs, check_vma=False)
```
